256 devices in a mesh: dp: 16 (over x, y), tensor: 16 (over z, core).
Axes of the slice: x: 4, y: 4, z: 8, core: 2. Of those that a mesh axis runs over, the one named last changes fastest.
Arguments:
- grad_out: bfloat16 [16384, 3584], P(('dp', 'tensor')), may hold values from -1.5 to 1.5
- pre_act: bfloat16 [2, 16384, 8192], P(None, 'dp', 'tensor'), may hold values from -6 to 6
- down_weight: bfloat16 [8192, 3584], P('tensor'), may hold values from -0.09375 to 0.09375
- error: bfloat16 [131072, 3584], P(('dp', 'tensor')), may hold values from -12 to 12
- q_start: float32 [512, 3584], P('tensor'), may hold values from -0.09375 to 0.09375
Outputs:
- grad_pre: bfloat16 [2, 16384, 8192], P(None, 'dp', 'tensor')
- new_error: bfloat16 [131072, 3584], P(('dp', 'tensor'))
- p_factor: float32 [32, 8192], P(None, 'tensor')
- q_factor: float32 [512, 3584], P('tensor')
The draws below stay inside these ranges and needn't reach their ends.
All inputs are finite; a program needn't handle non-finite values.
Results may differ from the reference program's by a relative error of at most 0.017.
Values may be sent and summed in bfloat16 or wider, within the bound.
No kernel may reach another device: no remote copies, remote signals or barrier semaphores. Data moves between devices by JAX's collectives and lax.ppermute only.
A program may use at most 128 MiB of HBM per device.

```python
import jax
import jax.numpy as jnp
from jax import lax

D = 3584
FF = 8192
RANK = 32
ROWS = 1024
TOKENS = 16384
N_DP = 16
N_TENSOR = 16


def levels(stream_key, extent, cuts, low, top_value):
    def one(position, blocks):
        steps = jax.random.uniform(jax.random.fold_in(jax.random.fold_in(stream_key, 6), position), (blocks,), jnp.float32, low / len(cuts), top_value / len(cuts))
        return jnp.repeat(jnp.exp(steps), extent[position] // blocks).reshape((-1,) + (1,) * (len(extent) - position - 1))

    level = one(*cuts[0])
    for cut in cuts[1:]:
        level = level * one(*cut)
    return level


def centred(stream_key, extent, deviation, bound, split=(), kind=jnp.bfloat16):
    array = deviation * jax.random.normal(stream_key, extent, jnp.float32)
    if split:
        array = array * levels(stream_key, extent, split, -0.22, 0.18)
    return jnp.clip(array, -bound, bound).astype(kind)


def setup_inputs(seed: int = 0) -> dict:
    arg_keys = jax.random.split(jax.random.key(seed), 6)
    grad_out = centred(arg_keys[0], (TOKENS, D), 0.25, 1.5, ((0, 256),))
    pre_act = centred(arg_keys[1], (2, TOKENS, FF), 1.0, 6.0, ((1, 16), (2, 16)))
    down_weight = centred(arg_keys[2], (FF, D), D ** -0.5, 0.09375, ((0, 16),))
    error = centred(arg_keys[3], (N_DP * FF, D), 2.0, 12.0, ((0, 256),))
    q_start = centred(arg_keys[4], (N_TENSOR * RANK, D), D ** -0.5, 0.09375, ((0, 16),), jnp.float32)
    return dict(grad_out=grad_out, pre_act=pre_act, down_weight=down_weight, error=error, q_start=q_start)


def gelu_pair(value):
    coeff = 0.7978845608028654
    tanh_val = jnp.tanh(coeff * (value + 0.044715 * value * value * value))
    gelu_value = 0.5 * value * (1.0 + tanh_val)
    gelu_slope = 0.5 * (1.0 + tanh_val) + 0.5 * value * (1.0 - tanh_val * tanh_val) * coeff * (1.0 + 3.0 * 0.044715 * value * value)
    return (gelu_value, gelu_slope)

def reference(grad_out, pre_act, down_weight, error, q_start):
    highest_precision = lax.Precision.HIGHEST
    gate_pre = pre_act[0].astype(jnp.float32)
    up_pre = pre_act[1].astype(jnp.float32)
    gelu_value, gelu_slope = gelu_pair(gate_pre)
    hidden = (gelu_value * up_pre).astype(jnp.bfloat16)
    hidden_grad = jnp.dot(grad_out.astype(jnp.float32), down_weight.T.astype(jnp.float32), preferred_element_type=jnp.float32)
    grad_pre = jnp.stack([hidden_grad * up_pre * gelu_slope, hidden_grad * gelu_value]).astype(jnp.bfloat16)
    shard = FF // N_TENSOR
    q_blocks = q_start.reshape(N_TENSOR, RANK, D)
    residual_errors = error.reshape(N_DP, FF, D)
    hid_ranks = hidden.reshape(N_DP, ROWS, FF)
    cot_ranks = grad_out.reshape(N_DP, ROWS, D)
    ranks = jnp.arange(N_DP, dtype=jnp.int32)

    def combined_product(compression_rank):
        weight_grad = jnp.dot(hid_ranks[compression_rank].T.astype(jnp.float32), cot_ranks[compression_rank].astype(jnp.float32), preferred_element_type=jnp.float32)
        return (weight_grad + residual_errors[compression_rank].astype(jnp.float32)).reshape(N_TENSOR, shard, D)

    def left_of(compression_rank):
        return jnp.einsum('tfd,trd->tfr', combined_product(compression_rank), q_blocks, precision=highest_precision)
    left = jnp.sum(lax.map(left_of, ranks), axis=0) / N_DP
    gram = jnp.einsum('tfr,tfs->trs', left, left, precision=highest_precision)
    chol_factor = jnp.linalg.cholesky(gram)
    orthonormal_left = jax.vmap(lambda low, mat: jax.scipy.linalg.solve_triangular(low, mat.T, lower=True))(chol_factor, left)

    def right_of(compression_rank):
        return jnp.einsum('och,ohe->oce', orthonormal_left, combined_product(compression_rank), precision=highest_precision)
    right_average = jnp.sum(lax.map(right_of, ranks), axis=0) / N_DP

    def error_of(compression_rank):
        lowrank_estimate = jnp.einsum('luk,lus->lks', orthonormal_left, right_average, precision=highest_precision)
        return (combined_product(compression_rank) - lowrank_estimate).astype(jnp.bfloat16).reshape(FF, D)
    new_error = lax.map(error_of, ranks).reshape(N_DP * FF, D)
    p_factor = orthonormal_left.transpose(1, 0, 2).reshape(RANK, FF)
    q_factor = right_average.reshape(N_TENSOR * RANK, D)
    return (grad_pre, new_error, p_factor, q_factor)
```

```python
import functools

import jax
import jax.numpy as jnp
from jax import lax
from jax.experimental import pallas as pl
from jax.experimental.pallas import tpu as pltpu
from jax.sharding import PartitionSpec as P

BF = jnp.bfloat16
F32 = jnp.float32
HI = lax.Precision.HIGHEST
DP = 16
NZ = 8
TOK = 64
CHIP = 2 * TOK
D = 3584
UNITS = 512
ROWS = 1024
RANK = 32
BLK = 512
NBLK = D // BLK
VMEM = 56 * 1024 * 1024


def gelu_pair(value):
    coeff = 0.7978845608028654
    tanh_val = jnp.tanh(coeff * (value + 0.044715 * value * value * value))
    gelu_value = 0.5 * value * (1.0 + tanh_val)
    gelu_slope = 0.5 * (1.0 + tanh_val) + 0.5 * value * (1.0 - tanh_val * tanh_val) * coeff * (
        1.0 + 3.0 * 0.044715 * value * value
    )
    return (gelu_value, gelu_slope)


def split(value, terms):
    parts = []
    for _ in range(terms):
        part = value.astype(BF)
        parts.append(part)
        value = value - part.astype(F32)
    return parts


def dot(a, b, ca, cb, precision=None):
    return lax.dot_general(
        a, b, (((ca,), (cb,)), ((), ())), preferred_element_type=F32, precision=precision
    )


def fold(stacked, terms):
    total = stacked[0:RANK]
    for k in range(1, terms):
        total = total + stacked[k * RANK : (k + 1) * RANK]
    return total


def step_z(value, k):
    return lax.ppermute(value, "tensor", [(i, (i + 2 * k) % (2 * NZ)) for i in range(2 * NZ)])


def other_core(value):
    return lax.ppermute(value, "tensor", [(i, i ^ 1) for i in range(2 * NZ)])


def step_xy(value, dx, dy):
    return lax.ppermute(
        value,
        "dp",
        [(4 * x + y, 4 * ((x + dx) % 4) + (y + dy) % 4) for x in range(4) for y in range(4)],
    )


def source_rows(z, core):
    rows = [z * CHIP + core * TOK, z * CHIP + (1 - core) * TOK]
    for s in (1, 2, 3):
        behind = lax.rem(z + NZ - s, NZ) * CHIP
        ahead = lax.rem(z + s, NZ) * CHIP
        rows += [behind + core * TOK, ahead + core * TOK]
        rows += [behind + (1 - core) * TOK, ahead + (1 - core) * TOK]
    return rows


def main_kernel(place, *refs):
    pieces = refs[:14]
    hidden_t, error, q3, merged, merged_b, left, tokens_out, tokens, g_acc, e_acc, sems, out_sem = refs[14:]
    i = pl.program_id(0)
    z, core = place[0], place[1]

    def copies():
        return [
            pltpu.make_async_copy(
                piece, tokens.at[pl.ds(pl.multiple_of(row, TOK), TOK), :], sems.at[k]
            )
            for k, (piece, row) in enumerate(zip(pieces, source_rows(z, core)))
        ]

    @pl.when(i == 0)
    def _():
        for copy in copies():
            copy.start()
        far = pl.multiple_of(lax.rem(z + 4, NZ) * CHIP, CHIP)
        tokens[pl.ds(far, CHIP), :] = jnp.zeros((CHIP, D), BF)
        g_acc[...] = jnp.zeros_like(g_acc)
        e_acc[...] = jnp.zeros_like(e_acc)
        for copy in copies():
            copy.wait()
        pltpu.make_async_copy(tokens, tokens_out, out_sem).start()

    columns = pl.ds(pl.multiple_of(i * BLK, BLK), BLK)
    block = tokens[:, columns]
    err = error[...]
    total = dot(hidden_t[...], block, 1, 0) + err.astype(F32)
    merged[...] = total
    merged_b[...] = total.astype(BF)
    q = q3[...]
    g_acc[...] += dot(q, block, 1, 1)
    e_acc[...] += dot(q, err, 1, 1)

    @pl.when(i == NBLK - 1)
    def _():
        g = jnp.concatenate(split(fold(g_acc[...], 3), 2), axis=0)
        left[...] = fold(e_acc[...], 3) + fold(dot(g, hidden_t[...], 1, 1), 2)
        pltpu.make_async_copy(tokens, tokens_out, out_sem).wait()


def main_call(place, pieces, hidden_t, error, q3):
    whole = lambda shape: pl.BlockSpec(shape, lambda i, p: (0, 0))
    cols = lambda rows: pl.BlockSpec((rows, BLK), lambda i, p: (0, i))
    return pl.pallas_call(
        main_kernel,
        grid_spec=pltpu.PrefetchScalarGridSpec(
            num_scalar_prefetch=1,
            grid=(NBLK,),
            in_specs=[pl.BlockSpec(memory_space=pl.ANY)] * 14
            + [whole((UNITS, ROWS)), cols(UNITS), cols(3 * RANK)],
            out_specs=[
                cols(UNITS),
                cols(UNITS),
                whole((RANK, UNITS)),
                pl.BlockSpec(memory_space=pl.ANY),
            ],
            scratch_shapes=[
                pltpu.VMEM((ROWS, D), BF),
                pltpu.VMEM((3 * RANK, ROWS), F32),
                pltpu.VMEM((3 * RANK, UNITS), F32),
                pltpu.SemaphoreType.DMA((14,)),
                pltpu.SemaphoreType.DMA,
            ],
        ),
        out_shape=[
            jax.ShapeDtypeStruct((UNITS, D), F32),
            jax.ShapeDtypeStruct((UNITS, D), BF),
            jax.ShapeDtypeStruct((RANK, UNITS), F32),
            jax.ShapeDtypeStruct((ROWS, D), BF),
        ],
        compiler_params=pltpu.CompilerParams(vmem_limit_bytes=VMEM),
        cost_estimate=pl.CostEstimate(
            flops=2 * ROWS * UNITS * D, bytes_accessed=30_000_000, transcendentals=0
        ),
        name="weight_grad",
    )(place, *pieces, hidden_t, error, q3)


def last_kernel(place, f4, b4, cf4, cb4, hidden_t, q3, left_in, left, last):
    core = place[1]
    half = TOK // 2
    mine = core * TOK
    theirs = (1 - core) * TOK
    last[pl.ds(pl.multiple_of(mine, half), half), :] = f4[...]
    last[pl.ds(pl.multiple_of(mine + half, half), half), :] = b4[...]
    last[pl.ds(pl.multiple_of(theirs, half), half), :] = cf4[...]
    last[pl.ds(pl.multiple_of(theirs + half, half), half), :] = cb4[...]
    far = pl.multiple_of(lax.rem(place[0] + 4, NZ) * CHIP, CHIP)
    g = jnp.concatenate(split(fold(dot(q3[...], last[...], 1, 1), 3), 2), axis=0)
    left[...] = left_in[...] + fold(dot(g, hidden_t[:, pl.ds(far, CHIP)], 1, 1), 2)


def last_call(place, f4, b4, cf4, cb4, hidden_t, q3, left_in):
    smem = pl.BlockSpec(memory_space=pltpu.SMEM)
    vmem = pl.BlockSpec(memory_space=pltpu.VMEM)
    return pl.pallas_call(
        last_kernel,
        in_specs=[smem] + [vmem] * 7,
        out_specs=[vmem] * 2,
        out_shape=[
            jax.ShapeDtypeStruct((RANK, UNITS), F32),
            jax.ShapeDtypeStruct((CHIP, D), BF),
        ],
        compiler_params=pltpu.CompilerParams(vmem_limit_bytes=VMEM),
        cost_estimate=pl.CostEstimate(flops=10**8, bytes_accessed=3_000_000, transcendentals=0),
        name="left_last",
    )(place, f4, b4, cf4, cb4, hidden_t, q3, left_in)


def right_kernel(place, l0, l1, l2, l3, hidden_t, last, merged_b, p_out, p3_out, right, p2, h2):
    i = pl.program_id(0)

    @pl.when(i == 0)
    def _():
        left = ((l0[...] + l2[...]) + (l1[...] + l3[...])) * (1.0 / DP)
        rest = dot(left, left, 1, 1, HI)
        rows = lax.broadcasted_iota(jnp.int32, (RANK, RANK), 0)
        inverse = (rows == lax.broadcasted_iota(jnp.int32, (RANK, RANK), 1)).astype(F32)
        for k in range(RANK):
            scale = lax.rsqrt(rest[k : k + 1, k : k + 1])
            column = jnp.where(rows[:, 0:1] > k, rest[:, k : k + 1] * scale, 0.0)
            rest_row = rest[k : k + 1, :] * scale
            inverse_row = inverse[k : k + 1, :] * scale
            rest = rest - column * rest_row
            inverse = jnp.where(rows == k, inverse_row, inverse - column * inverse_row)
        factor = dot(inverse, left, 1, 0, HI)
        p_out[...] = factor
        high, low = split(factor, 2)
        p2[...] = jnp.concatenate([high, low], axis=0)
        p3_out[...] = jnp.concatenate([high, low, high], axis=0)
        far = pl.multiple_of(lax.rem(place[0] + 4, NZ) * CHIP, CHIP)
        mine = fold(dot(p2[...], hidden_t[:, pl.ds(far, CHIP)], 1, 0), 2)
        h2[...] = jnp.concatenate(split(mine, 2), axis=0)

    total = dot(p2[...], merged_b[...], 1, 0) + dot(h2[...], last[...], 1, 0)
    right[...] = fold(total, 2).astype(BF)


def right_call(place, lefts, hidden_t, last, merged_b):
    whole = lambda shape: pl.BlockSpec(shape, lambda i, p: (0, 0))
    cols = lambda rows: pl.BlockSpec((rows, BLK), lambda i, p: (0, i))
    return pl.pallas_call(
        right_kernel,
        grid_spec=pltpu.PrefetchScalarGridSpec(
            num_scalar_prefetch=1,
            grid=(NBLK,),
            in_specs=[whole((RANK, UNITS))] * 4
            + [whole((UNITS, ROWS)), cols(CHIP), cols(UNITS)],
            out_specs=[whole((RANK, UNITS)), whole((3 * RANK, UNITS)), cols(RANK)],
            scratch_shapes=[pltpu.VMEM((2 * RANK, UNITS), BF), pltpu.VMEM((2 * RANK, CHIP), BF)],
        ),
        out_shape=[
            jax.ShapeDtypeStruct((RANK, UNITS), F32),
            jax.ShapeDtypeStruct((3 * RANK, UNITS), BF),
            jax.ShapeDtypeStruct((RANK, D), BF),
        ],
        compiler_params=pltpu.CompilerParams(vmem_limit_bytes=VMEM),
        cost_estimate=pl.CostEstimate(flops=10**8, bytes_accessed=6_000_000, transcendentals=0),
        name="right_factor",
    )(place, *lefts, hidden_t, last, merged_b)


def error_kernel(place, p3, hidden_t, last, merged, q, out, p3_t, h_last):
    @pl.when(pl.program_id(0) == 0)
    def _():
        p3_t[...] = jnp.transpose(p3[...].astype(F32)).astype(BF)
        far = pl.multiple_of(lax.rem(place[0] + 4, NZ) * CHIP, CHIP)
        h_last[...] = hidden_t[:, pl.ds(far, CHIP)]

    high, low = split(q[...], 2)
    q3 = jnp.concatenate([high, high, low], axis=0)
    total = merged[...] + dot(h_last[...], last[...], 1, 0) - dot(p3_t[...], q3, 1, 0)
    out[...] = total.astype(BF)


def error_call(place, p3, hidden_t, last, merged, q):
    whole = lambda shape: pl.BlockSpec(shape, lambda i, p: (0, 0))
    cols = lambda rows: pl.BlockSpec((rows, BLK), lambda i, p: (0, i))
    return pl.pallas_call(
        error_kernel,
        grid_spec=pltpu.PrefetchScalarGridSpec(
            num_scalar_prefetch=1,
            grid=(NBLK,),
            in_specs=[
                whole((3 * RANK, UNITS)),
                whole((UNITS, ROWS)),
                cols(CHIP),
                cols(UNITS),
                cols(RANK),
            ],
            out_specs=cols(UNITS),
            scratch_shapes=[pltpu.VMEM((UNITS, 3 * RANK), BF), pltpu.VMEM((UNITS, CHIP), BF)],
        ),
        out_shape=jax.ShapeDtypeStruct((UNITS, D), BF),
        compiler_params=pltpu.CompilerParams(vmem_limit_bytes=VMEM),
        cost_estimate=pl.CostEstimate(flops=10**9, bytes_accessed=12_000_000, transcendentals=0),
        name="new_error",
    )(place, p3, hidden_t, last, merged, q)


TBLK = 256


def pre_kernel(place, tokens, last, weight, pre, out, grad):
    i = pl.program_id(0)
    far = lax.rem(place[0] + 4, NZ)
    grad[...] = dot(tokens[...], weight[...], 1, 1)

    @pl.when(i == far // 2)
    def _():
        row = pl.multiple_of(lax.rem(far, 2) * CHIP, CHIP)
        grad[pl.ds(row, CHIP), :] = dot(last[...], weight[...], 1, 1)

    up = pre[1].astype(F32)
    value, slope = gelu_pair(pre[0].astype(F32))
    out[0] = (grad[...] * up * slope).astype(BF)
    out[1] = (grad[...] * value).astype(BF)


def pre_call(place, tokens, last, weight, pre):
    whole = lambda shape: pl.BlockSpec(shape, lambda i, p: (0, 0))
    return pl.pallas_call(
        pre_kernel,
        grid_spec=pltpu.PrefetchScalarGridSpec(
            num_scalar_prefetch=1,
            grid=(ROWS // TBLK,),
            in_specs=[
                pl.BlockSpec((TBLK, D), lambda i, p: (i, 0)),
                whole((CHIP, D)),
                whole((UNITS, D)),
                pl.BlockSpec((2, TBLK, UNITS), lambda i, p: (0, i, 0)),
            ],
            out_specs=pl.BlockSpec((2, TBLK, UNITS), lambda i, p: (0, i, 0)),
            scratch_shapes=[pltpu.VMEM((TBLK, UNITS), F32)],
        ),
        out_shape=jax.ShapeDtypeStruct((2, ROWS, UNITS), BF),
        compiler_params=pltpu.CompilerParams(vmem_limit_bytes=VMEM),
        cost_estimate=pl.CostEstimate(
            flops=2 * ROWS * UNITS * D, bytes_accessed=16_000_000, transcendentals=0
        ),
        name="grad_pre",
    )(place, tokens, last, weight, pre)


def sum_of_four(a, b, c, d):
    return (a + c) + (b + d)


def on_device(grad_out, pre_act, down_weight, error, q_start):
    index = lax.axis_index("tensor")
    place = jnp.stack([index // 2, lax.rem(index, 2)]).astype(jnp.int32)

    gelu_value, _ = gelu_pair(pre_act[0].astype(F32))
    hidden_t = (gelu_value * pre_act[1].astype(F32)).astype(BF).T
    q3 = jnp.concatenate(split(q_start, 3), axis=0)

    pieces = [grad_out, other_core(grad_out)]
    ahead = behind = grad_out
    for _ in range(3):
        behind, ahead = step_z(behind, 1), step_z(ahead, -1)
        pieces += [behind, ahead, other_core(behind), other_core(ahead)]
    half = TOK // 2
    behind, ahead = step_z(behind[:half], 1), step_z(ahead[half:], -1)

    merged, merged_b, left, tokens = main_call(place, pieces, hidden_t, error, q3)
    left, last = last_call(
        place, behind, ahead, other_core(behind), other_core(ahead), hidden_t, q3, left
    )

    left = sum_of_four(left, *[step_xy(left, k, 0) for k in (1, 2, 3)])
    lefts = [left] + [step_xy(left, 0, k) for k in (1, 2, 3)]
    grad_pre = pre_call(place, tokens, last, down_weight, pre_act)
    p_factor, p3, right = right_call(place, lefts, hidden_t, last, merged_b)

    parts = lax.all_to_all(right.reshape(DP, RANK // DP, D), "dp", 0, 0, tiled=True)
    mine = jnp.sum(parts.astype(F32), axis=0).astype(BF)
    right = lax.all_to_all(
        jnp.broadcast_to(mine[None], (DP, RANK // DP, D)), "dp", 0, 0, tiled=True
    ).reshape(RANK, D)
    q_factor = right.astype(F32) * (1.0 / DP)
    new_error = error_call(place, p3, hidden_t, last, merged, q_factor)
    return (grad_pre, new_error, p_factor, q_factor)


def solution(mesh):
    placed = (
        P(("dp", "tensor"), None),
        P(None, "dp", "tensor"),
        P("tensor", None),
        P(("dp", "tensor"), None),
        P("tensor", None),
    )
    return jax.shard_map(
        on_device,
        mesh=mesh,
        in_specs=placed,
        out_specs=(
            P(None, "dp", "tensor"),
            P(("dp", "tensor"), None),
            P(None, "tensor"),
            P("tensor", None),
        ),
        check_vma=False,
    )
```

```python
import functools

import jax
import jax.numpy as jnp
from jax import lax
from jax.experimental import pallas as pl
from jax.experimental.pallas import tpu as pltpu
from jax.sharding import PartitionSpec as P

BF = jnp.bfloat16
F32 = jnp.float32
HI = lax.Precision.HIGHEST
DP = 16
NZ = 8
TOK = 64
CHIP = 2 * TOK
D = 3584
UNITS = 512
ROWS = 1024
EARLY = 5 * CHIP
RANK = 32
BLK = 512
NBLK = D // BLK
MIB = 1024 * 1024


def gelu_pair(value):
    coeff = 0.7978845608028654
    tanh_val = jnp.tanh(coeff * (value + 0.044715 * value * value * value))
    gelu_value = 0.5 * value * (1.0 + tanh_val)
    gelu_slope = 0.5 * (1.0 + tanh_val) + 0.5 * value * (1.0 - tanh_val * tanh_val) * coeff * (
        1.0 + 3.0 * 0.044715 * value * value
    )
    return (gelu_value, gelu_slope)


def split(value, terms):
    parts = []
    for _ in range(terms):
        part = value.astype(BF)
        parts.append(part)
        value = value - part.astype(F32)
    return parts


def split_exactly(value, terms):
    parts = []
    for _ in range(terms):
        part = lax.reduce_precision(value, 8, 7)
        parts.append(part.astype(BF))
        value = value - part
    return parts


def dot(a, b, ca, cb, precision=None):
    return lax.dot_general(
        a, b, (((ca,), (cb,)), ((), ())), preferred_element_type=F32, precision=precision
    )


def fold(stacked, terms):
    total = stacked[0:RANK]
    for k in range(1, terms):
        total = total + stacked[k * RANK : (k + 1) * RANK]
    return total


def chip_of(slot, z):
    return lax.rem(z + jnp.where(slot % 2 == 1, 2 * NZ - (slot + 1) // 2, NZ + slot // 2), NZ)


def rows_of_step(s, core):
    if s == 0:
        return [core * TOK, (1 - core) * TOK]
    if s == 4:
        return [(14 + core) * TOK, (15 - core) * TOK]
    return [
        (4 * s - 2 + 3 * core) * TOK,
        (4 * s - 1 + core) * TOK,
        (4 * s + 1 - 3 * core) * TOK,
        (4 * s - core) * TOK,
    ]


def after(value, *others):
    return lax.optimization_barrier((value,) + others)[0]


def other_core(value):
    return lax.ppermute(value, "tensor", [(i, i ^ 1) for i in range(2 * NZ)])


def along_z(value):
    return lax.ppermute(
        value, "tensor", [(i, (i + 2 - 4 * (i % 2)) % (2 * NZ)) for i in range(2 * NZ)]
    )


def sum_over_ring(value, turn):
    def pairs(k):
        for i in range(DP * 2 * NZ):
            dp, t = divmod(i, 2 * NZ)
            x, y = divmod(dp, 4)
            if (t + turn) % 2 == 0:
                x = (x + k) % 4
            else:
                y = (y + k) % 4
            yield (i, (4 * x + y) * 2 * NZ + t)

    return [value] + [lax.ppermute(value, ("dp", "tensor"), list(pairs(k))) for k in (1, 2, 3)]


def sum_of_four(a, b, c, d):
    return (a + c) + (b + d)


SMEM = pl.BlockSpec(memory_space=pltpu.SMEM)
WHOLE = pl.BlockSpec(memory_space=pltpu.VMEM)


def kept(shape, dtype):
    return pltpu.VMEM(shape, dtype)


def held(value):
    return pltpu.with_memory_space_constraint(value, pltpu.VMEM)


def kept_out(shape, dtype):
    return pltpu.HBM(shape, dtype)


def from_hbm(value):
    return pltpu.with_memory_space_constraint(value, pltpu.HBM)


def params(mib):
    return pltpu.CompilerParams(vmem_limit_bytes=mib * MIB)


def cost(flops, moved):
    return pl.CostEstimate(flops=flops, bytes_accessed=moved, transcendentals=0)


def hidden_kernel(place, pre, hidden_t):
    value, _ = gelu_pair(pre[0].astype(F32))
    hidden = (value * pre[1].astype(F32)).astype(BF).astype(F32)
    hidden_t[...] = jnp.transpose(hidden).astype(BF)


def hidden_call(place, pre):
    return pl.pallas_call(
        hidden_kernel,
        grid_spec=pltpu.PrefetchScalarGridSpec(
            num_scalar_prefetch=1,
            grid=(NZ,),
            in_specs=[pl.BlockSpec((2, CHIP, UNITS), lambda i, p: (0, chip_of(i, p[0]), 0))],
            out_specs=pl.BlockSpec((UNITS, CHIP), lambda i, p: (0, i)),
        ),
        out_shape=kept((UNITS, ROWS), BF),
        compiler_params=params(8),
        cost_estimate=cost(10**7, 3_000_000),
        name="hidden",
    )(place, pre)


def main_kernel(place, *refs):
    pieces = refs[:10]
    hidden_t, error, q3, merged, left, tokens, g_acc, e_acc = refs[10:]
    i = pl.program_id(0)
    rows = [r for s in range(3) for r in rows_of_step(s, place[1])]
    for piece, row in zip(pieces, rows):
        tokens[pl.ds(pl.multiple_of(row, TOK), TOK), :] = piece[...]

    @pl.when(i == 0)
    def _():
        g_acc[...] = jnp.zeros_like(g_acc)
        e_acc[...] = jnp.zeros_like(e_acc)

    block = tokens[...]
    err = error[...]
    merged[...] = (dot(hidden_t[:, :EARLY], block, 1, 0) + err.astype(F32)).astype(BF)
    q = q3[...]
    g_acc[...] += dot(q, block, 1, 1)
    e_acc[...] += dot(q, err, 1, 1)

    @pl.when(i == NBLK - 1)
    def _():
        g = jnp.concatenate(split(fold(g_acc[...], 3), 2), axis=0)
        left[...] = fold(e_acc[...], 3) + fold(dot(g, hidden_t[:, :EARLY], 1, 1), 2)


def main_call(place, pieces, hidden_t, error, q3):
    whole = lambda shape: pl.BlockSpec(shape, lambda i, p: (0, 0))
    cols = lambda rows: pl.BlockSpec((rows, BLK), lambda i, p: (0, i))
    return pl.pallas_call(
        main_kernel,
        grid_spec=pltpu.PrefetchScalarGridSpec(
            num_scalar_prefetch=1,
            grid=(NBLK,),
            in_specs=[cols(TOK)] * 10
            + [whole((UNITS, ROWS)), cols(UNITS), cols(3 * RANK)],
            out_specs=[cols(UNITS), whole((RANK, UNITS))],
            scratch_shapes=[
                pltpu.VMEM((EARLY, BLK), BF),
                pltpu.VMEM((3 * RANK, EARLY), F32),
                pltpu.VMEM((3 * RANK, UNITS), F32),
            ],
        ),
        out_shape=[
            kept((UNITS, D), BF),
            jax.ShapeDtypeStruct((RANK, UNITS), F32),
        ],
        compiler_params=params(14),
        cost_estimate=cost(2 * EARLY * UNITS * D, 14_000_000),
        name="weight_grad",
    )(place, *map(held, pieces), held(hidden_t), error, q3)


def left_kernel(step, place, *refs):
    pieces = refs[:-5]
    hidden_t, q3, left_in, left, last = refs[-5:]
    base = (5 if step == 3 else 7) * CHIP
    for piece, row in zip(pieces, rows_of_step(step, place[1])):
        last[pl.ds(pl.multiple_of(row - base, TOK), TOK), :] = piece[...]
    g = fold(dot(q3[...], last[...], 1, 1), 3)
    g = jnp.concatenate(split(g, 2), axis=0)
    here = hidden_t[:, base : base + last.shape[0]]
    left[...] = left_in[...] + fold(dot(g, here, 1, 1), 2)


def left_call(step, place, pieces, hidden_t, q3, left_in):
    rows = TOK * len(pieces)
    return pl.pallas_call(
        functools.partial(left_kernel, step),
        in_specs=[SMEM] + [WHOLE] * (len(pieces) + 3),
        out_specs=[WHOLE] * 2,
        out_shape=[
            jax.ShapeDtypeStruct((RANK, UNITS), F32),
            kept((rows, D), BF),
        ],
        compiler_params=params(12),
        cost_estimate=cost(2 * rows * D * 96, 4_000_000),
        name="left_of_step",
    )(place, *map(held, pieces), held(hidden_t), held(q3), left_in)


def right_kernel(l0, l1, l2, l3, hidden_t, last_a, last_b, merged, p_out, right):
    left = ((l0[...] + l2[...]) + (l1[...] + l3[...])) * (1.0 / DP)
    rest = dot(left, left, 1, 1, HI)
    rows = lax.broadcasted_iota(jnp.int32, (RANK, RANK), 0)
    inverse = (rows == lax.broadcasted_iota(jnp.int32, (RANK, RANK), 1)).astype(F32)
    for k in range(RANK):
        scale = lax.rsqrt(rest[k : k + 1, k : k + 1])
        column = jnp.where(rows[:, 0:1] > k, rest[:, k : k + 1] * scale, 0.0)
        rest_row = rest[k : k + 1, :] * scale
        inverse_row = inverse[k : k + 1, :] * scale
        rest = rest - column * rest_row
        inverse = jnp.where(rows == k, inverse_row, inverse - column * inverse_row)
    factor = dot(inverse, left, 1, 0, HI)
    p_out[...] = factor
    high, low = split(factor, 2)
    p2 = jnp.concatenate([high, low], axis=0)
    mine = fold(dot(p2, hidden_t[:, EARLY:], 1, 0), 2)
    h2 = jnp.concatenate(split(mine, 2), axis=0)
    for i in range(NBLK):
        c = slice(i * BLK, (i + 1) * BLK)
        total = dot(p2, merged[:, c], 1, 0)
        total += dot(h2[:, : 2 * CHIP], last_a[:, c], 1, 0)
        total += dot(h2[:, 2 * CHIP :], last_b[:, c], 1, 0)
        right[:, c] = fold(total, 2).astype(BF)


def right_call(lefts, hidden_t, last_a, last_b, merged):
    return pl.pallas_call(
        right_kernel,
        in_specs=[WHOLE] * 8,
        out_specs=[WHOLE] * 2,
        out_shape=[
            jax.ShapeDtypeStruct((RANK, UNITS), F32),
            jax.ShapeDtypeStruct((RANK, D), BF),
        ],
        compiler_params=params(14),
        cost_estimate=cost(10**8, 8_000_000),
        name="right_factor",
    )(*lefts, held(hidden_t), held(last_a), held(last_b), held(merged))


def sum_kernel(parts, out):
    total = jnp.sum(parts[...].astype(F32), axis=0, keepdims=True)
    out[...] = jnp.broadcast_to(total.astype(BF), out.shape)


def sum_call(parts):
    return pl.pallas_call(
        sum_kernel,
        in_specs=[WHOLE],
        out_specs=WHOLE,
        out_shape=jax.ShapeDtypeStruct(parts.shape, BF),
        compiler_params=params(8),
        cost_estimate=cost(10**6, 500_000),
        name="sum_of_ranks",
    )(parts)


HALF = D // 2
WIDE = HALF // 2


def merge_kernel(hidden_t, last_a, last_b, merged, total):
    part = merged[...].astype(F32)
    part += dot(hidden_t[:, EARLY : EARLY + 2 * CHIP], last_a[...], 1, 0)
    part += dot(hidden_t[:, EARLY + 2 * CHIP :], last_b[...], 1, 0)
    total[...] = part.astype(BF)


def merge_call(half, hidden_t, last_a, last_b, merged):
    first = half * (HALF // WIDE)
    cols = lambda rows: pl.BlockSpec((rows, WIDE), lambda i: (0, first + i))
    return pl.pallas_call(
        merge_kernel,
        grid=(HALF // WIDE,),
        in_specs=[
            pl.BlockSpec((UNITS, ROWS), lambda i: (0, 0)),
            cols(2 * CHIP),
            cols(CHIP),
            cols(UNITS),
        ],
        out_specs=pl.BlockSpec((UNITS, WIDE), lambda i: (0, i)),
        out_shape=kept_out((UNITS, HALF), BF),
        compiler_params=params(14),
        cost_estimate=cost(3 * CHIP * UNITS * D, 6_000_000),
        name="weight_grad_rest",
    )(*map(from_hbm, (hidden_t, last_a, last_b, merged)))


def error_kernel(factor, lower, upper, q, out, p2_t):
    i = pl.program_id(0)

    @pl.when(i == 0)
    def _():
        p2_t[...] = jnp.concatenate(split(jnp.transpose(factor[...]), 2), axis=1)

    rounded = q[...].astype(BF)
    rounded = jnp.concatenate([rounded, rounded], axis=0)
    estimate = dot(p2_t[...], rounded, 1, 0)

    @pl.when(i < HALF // WIDE)
    def _():
        out[...] = (lower[...].astype(F32) - estimate).astype(BF)

    @pl.when(i >= HALF // WIDE)
    def _():
        out[...] = (upper[...].astype(F32) - estimate).astype(BF)


def error_call(factor, lower, upper, q):
    per = HALF // WIDE
    cols = lambda rows: pl.BlockSpec((rows, WIDE), lambda i: (0, i))
    return pl.pallas_call(
        error_kernel,
        grid=(D // WIDE,),
        in_specs=[
            pl.BlockSpec((RANK, UNITS), lambda i: (0, 0)),
            pl.BlockSpec((UNITS, WIDE), lambda i: (0, jnp.minimum(i, per - 1))),
            pl.BlockSpec((UNITS, WIDE), lambda i: (0, jnp.maximum(i - per, 0))),
            cols(RANK),
        ],
        out_specs=cols(UNITS),
        scratch_shapes=[pltpu.VMEM((UNITS, 2 * RANK), BF)],
        out_shape=jax.ShapeDtypeStruct((UNITS, D), BF),
        compiler_params=params(12),
        cost_estimate=cost(2 * 64 * UNITS * D, 8_000_000),
        name="new_error",
    )(factor, from_hbm(lower), from_hbm(upper), q)


def slots_of_step(s):
    return {0: [0], 4: [7]}.get(s, [2 * s - 1, 2 * s])


def finish_pre(grad, pre, stage):
    value, slope = gelu_pair(pre[0].astype(F32))
    stage[0] = (grad * pre[1].astype(F32) * slope).astype(BF)
    stage[1] = (grad * value).astype(BF)


def pre_kernel(s, place, *refs):
    slots = slots_of_step(s)
    count = 2 * len(slots) if s < 3 else 1
    pieces, refs = refs[:count], refs[count:]
    pres, refs = refs[: len(slots)], refs[len(slots) :]
    weight, (out, tokens, stage, sems) = refs[0], refs[-4:]
    if s < 3:
        for piece, row in zip(pieces, rows_of_step(s, place[1])):
            row = pl.multiple_of(row - slots[0] * CHIP, TOK)
            tokens[pl.ds(row, TOK), :] = piece[...]
        here = tokens[...]
    else:
        here = pieces[0][...]
    grad = dot(here, weight[...], 1, 1)
    copies = []
    for k, slot in enumerate(slots):
        finish_pre(grad[k * CHIP : (k + 1) * CHIP], pres[k], stage.at[k])
        row = pl.multiple_of(chip_of(slot, place[0]) * CHIP, CHIP)
        copies.append(
            pltpu.make_async_copy(stage.at[k], out.at[:, pl.ds(row, CHIP), :], sems.at[k])
        )
        copies[-1].start()
    for copy in copies:
        copy.wait()


def pre_call(s, place, pieces, pre, weight, so_far=None):
    slots = slots_of_step(s)
    chip = lambda slot: pl.BlockSpec((2, CHIP, UNITS), lambda i, p: (0, chip_of(slot, p[0]), 0))
    any_space = pl.BlockSpec(memory_space=pl.ANY)
    specs = [WHOLE] * len(pieces) + [chip(k) for k in slots] + [WHOLE]
    args = [place, *map(held, pieces), *([pre] * len(slots)), held(weight)]
    aliases = {}
    if so_far is not None:
        aliases = {len(args): 0}
        specs.append(any_space)
        args.append(so_far)
    rows = CHIP * len(slots)
    return pl.pallas_call(
        functools.partial(pre_kernel, s),
        grid_spec=pltpu.PrefetchScalarGridSpec(
            num_scalar_prefetch=1,
            grid=(1,),
            in_specs=specs,
            out_specs=any_space,
            scratch_shapes=[
                pltpu.VMEM((rows, D), BF),
                pltpu.VMEM((len(slots), 2, CHIP, UNITS), BF),
                pltpu.SemaphoreType.DMA((len(slots),)),
            ],
        ),
        out_shape=jax.ShapeDtypeStruct((2, ROWS, UNITS), BF),
        input_output_aliases=aliases,
        compiler_params=params(10),
        cost_estimate=cost(2 * rows * UNITS * D, 2 * rows * D + 8 * rows * UNITS),
        name="grad_pre",
    )(*args)


def on_device(grad_out, pre_act, down_weight, error, q_start):
    index = lax.axis_index("tensor").astype(jnp.int32)
    place = jnp.stack([index >> 1, index & 1])
    hidden_t = hidden_call(place, pre_act)
    q3 = jnp.concatenate(split_exactly(q_start, 3), axis=0)


    def pre_of(step, pieces, so_far=None):
        return pre_call(step, place, pieces, pre_act, down_weight, so_far)

    a0, b0 = grad_out, other_core(grad_out)
    a1, b1 = along_z(a0), along_z(after(b0, hidden_t))
    a2 = along_z(a1)
    grad_pre = pre_of(0, [a0, after(b0, a1)])
    b2 = along_z(after(b1, a1, grad_pre))
    xa1, xb1 = other_core(after(a1, b1, grad_pre)), other_core(after(b1, a1, grad_pre))
    grad_pre = pre_of(1, [a1, b1, xa1, xb1], grad_pre)
    a3 = along_z(after(a2, b1, grad_pre))
    b3 = along_z(after(b2, a2, grad_pre))
    xa2, xb2 = other_core(after(a2, b2, grad_pre)), other_core(after(b2, a2, grad_pre))
    grad_pre = pre_of(2, [a2, b2, xa2, xb2], grad_pre)
    a4 = along_z(after(a3, b2, grad_pre))
    early = [a0, b0, a1, b1, xa1, xb1, a2, b2, xa2, after(xb2, a3)]
    merged, left = main_call(place, early, hidden_t, error, q3)
    xa3, xb3 = other_core(after(a3, b3, left)), other_core(after(b3, a3, left))
    left, last_a = left_call(3, place, [a3, b3, xa3, xb3], hidden_t, q3, left)
    xa4 = other_core(after(a4, b3))
    left, last_b = left_call(4, place, [a4, xa4], hidden_t, q3, left)

    grad_pre = pre_of(3, [after(last_a, left)], grad_pre)
    lefts = sum_over_ring(left, 0)
    left = sum_of_four(lefts[0], lefts[1], lefts[2], after(lefts[3], grad_pre))
    grad_pre = pre_of(4, [after(last_b, left)], grad_pre)
    lefts = sum_over_ring(left, 1)
    lefts[3] = after(lefts[3], grad_pre)
    p_factor, right = right_call(lefts, hidden_t, last_a, last_b, merged)

    parts = lax.all_to_all(right.reshape(DP, RANK // DP, D), "dp", 0, 0, tiled=True)
    lower = merge_call(0, after(hidden_t, right), last_a, last_b, merged)
    summed = sum_call(after(parts, lower))
    right = lax.all_to_all(summed, "dp", 0, 0, tiled=True).reshape(RANK, D)
    upper = merge_call(1, after(hidden_t, summed), last_a, last_b, merged)
    q_factor = right.astype(F32) * (1.0 / DP)
    new_error = error_call(p_factor, lower, upper, q_factor)
    return (grad_pre, new_error, p_factor, q_factor)


def solution(mesh):
    placed = (
        P(("dp", "tensor"), None),
        P(None, "dp", "tensor"),
        P("tensor", None),
        P(("dp", "tensor"), None),
        P("tensor", None),
    )
    return jax.shard_map(
        on_device,
        mesh=mesh,
        in_specs=placed,
        out_specs=(
            P(None, "dp", "tensor"),
            P(("dp", "tensor"), None),
            P(None, "tensor"),
            P("tensor", None),
        ),
        check_vma=False,
    )
```

```python
import functools

import jax
import jax.numpy as jnp
from jax import lax
from jax.experimental import pallas as pl
from jax.experimental.pallas import tpu as pltpu
from jax.sharding import PartitionSpec as P

BF = jnp.bfloat16
F32 = jnp.float32
HI = lax.Precision.HIGHEST
DP = 16
NZ = 8
TOK = 64
CHIP = 2 * TOK
D = 3584
UNITS = 512
ROWS = 1024
EARLY = 5 * CHIP
RANK = 32
BLK = 512
NBLK = D // BLK
MIB = 1024 * 1024


def gelu_pair(value):
    coeff = 0.7978845608028654
    tanh_val = jnp.tanh(coeff * (value + 0.044715 * value * value * value))
    gelu_value = 0.5 * value * (1.0 + tanh_val)
    gelu_slope = 0.5 * (1.0 + tanh_val) + 0.5 * value * (1.0 - tanh_val * tanh_val) * coeff * (
        1.0 + 3.0 * 0.044715 * value * value
    )
    return (gelu_value, gelu_slope)


def split(value, terms):
    parts = []
    for _ in range(terms):
        part = value.astype(BF)
        parts.append(part)
        value = value - part.astype(F32)
    return parts


def split_exactly(value, terms):
    parts = []
    for _ in range(terms):
        part = lax.reduce_precision(value, 8, 7)
        parts.append(part.astype(BF))
        value = value - part
    return parts


def dot(a, b, ca, cb, precision=None):
    return lax.dot_general(
        a, b, (((ca,), (cb,)), ((), ())), preferred_element_type=F32, precision=precision
    )


def fold(stacked, terms):
    total = stacked[0:RANK]
    for k in range(1, terms):
        total = total + stacked[k * RANK : (k + 1) * RANK]
    return total


def chip_of(slot, z):
    return lax.rem(z + jnp.where(slot % 2 == 1, 2 * NZ - (slot + 1) // 2, NZ + slot // 2), NZ)


def rows_of_step(s, core):
    if s == 0:
        return [core * TOK, (1 - core) * TOK]
    if s == 4:
        return [(14 + core) * TOK, (15 - core) * TOK]
    return [
        (4 * s - 2 + 3 * core) * TOK,
        (4 * s - 1 + core) * TOK,
        (4 * s + 1 - 3 * core) * TOK,
        (4 * s - core) * TOK,
    ]


def after(value, *others):
    return lax.optimization_barrier((value,) + others)[0]


def other_core(value):
    return lax.ppermute(value, "tensor", [(i, i ^ 1) for i in range(2 * NZ)])


def along_z(value):
    return lax.ppermute(
        value, "tensor", [(i, (i + 2 - 4 * (i % 2)) % (2 * NZ)) for i in range(2 * NZ)]
    )


def sum_over_ring(value, turn):
    def pairs(k):
        for i in range(DP * 2 * NZ):
            dp, t = divmod(i, 2 * NZ)
            x, y = divmod(dp, 4)
            if (t + turn) % 2 == 0:
                x = (x + k) % 4
            else:
                y = (y + k) % 4
            yield (i, (4 * x + y) * 2 * NZ + t)

    return [value] + [lax.ppermute(value, ("dp", "tensor"), list(pairs(k))) for k in (1, 2, 3)]


def sum_of_four(a, b, c, d):
    return (a + c) + (b + d)


SMEM = pl.BlockSpec(memory_space=pltpu.SMEM)
WHOLE = pl.BlockSpec(memory_space=pltpu.VMEM)


def kept(shape, dtype):
    return pltpu.VMEM(shape, dtype)


def held(value):
    return pltpu.with_memory_space_constraint(value, pltpu.VMEM)


def kept_out(shape, dtype):
    return pltpu.HBM(shape, dtype)


def from_hbm(value):
    return pltpu.with_memory_space_constraint(value, pltpu.HBM)


def params(mib):
    return pltpu.CompilerParams(vmem_limit_bytes=mib * MIB)


def cost(flops, moved):
    return pl.CostEstimate(flops=flops, bytes_accessed=moved, transcendentals=0)


SHORT = cost(10**6, 10**5)


def hidden_kernel(place, pre, hidden_t):
    value, _ = gelu_pair(pre[0].astype(F32))
    hidden = (value * pre[1].astype(F32)).astype(BF).astype(F32)
    hidden_t[...] = jnp.transpose(hidden).astype(BF)


def hidden_call(place, pre):
    return pl.pallas_call(
        hidden_kernel,
        grid_spec=pltpu.PrefetchScalarGridSpec(
            num_scalar_prefetch=1,
            grid=(NZ,),
            in_specs=[pl.BlockSpec((2, CHIP, UNITS), lambda i, p: (0, chip_of(i, p[0]), 0))],
            out_specs=pl.BlockSpec((UNITS, CHIP), lambda i, p: (0, i)),
        ),
        out_shape=kept((UNITS, ROWS), BF),
        compiler_params=params(8),
        cost_estimate=SHORT,
        name="hidden",
    )(place, pre)


def main_kernel(place, *refs):
    pieces = refs[:10]
    hidden_t, error, q3, merged, left, tokens, g_acc, e_acc = refs[10:]
    i = pl.program_id(0)
    rows = [r for s in range(3) for r in rows_of_step(s, place[1])]
    for piece, row in zip(pieces, rows):
        tokens[pl.ds(pl.multiple_of(row, TOK), TOK), :] = piece[...]

    @pl.when(i == 0)
    def _():
        g_acc[...] = jnp.zeros_like(g_acc)
        e_acc[...] = jnp.zeros_like(e_acc)

    block = tokens[...]
    err = error[...]
    merged[...] = (dot(hidden_t[:, :EARLY], block, 1, 0) + err.astype(F32)).astype(BF)
    q = q3[...]
    g_acc[...] += dot(q, block, 1, 1)
    e_acc[...] += dot(q, err, 1, 1)

    @pl.when(i == NBLK - 1)
    def _():
        g = jnp.concatenate(split(fold(g_acc[...], 3), 2), axis=0)
        left[...] = fold(e_acc[...], 3) + fold(dot(g, hidden_t[:, :EARLY], 1, 1), 2)


def main_call(place, pieces, hidden_t, error, q3):
    whole = lambda shape: pl.BlockSpec(shape, lambda i, p: (0, 0))
    cols = lambda rows: pl.BlockSpec((rows, BLK), lambda i, p: (0, i))
    return pl.pallas_call(
        main_kernel,
        grid_spec=pltpu.PrefetchScalarGridSpec(
            num_scalar_prefetch=1,
            grid=(NBLK,),
            in_specs=[cols(TOK)] * 10
            + [whole((UNITS, ROWS)), cols(UNITS), cols(3 * RANK)],
            out_specs=[cols(UNITS), whole((RANK, UNITS))],
            scratch_shapes=[
                pltpu.VMEM((EARLY, BLK), BF),
                pltpu.VMEM((3 * RANK, EARLY), F32),
                pltpu.VMEM((3 * RANK, UNITS), F32),
            ],
        ),
        out_shape=[
            kept((UNITS, D), BF),
            jax.ShapeDtypeStruct((RANK, UNITS), F32),
        ],
        compiler_params=params(14),
        cost_estimate=SHORT,
        name="weight_grad",
    )(place, *map(held, pieces), held(hidden_t), error, q3)


def left_kernel(step, place, *refs):
    pieces = refs[:-5]
    hidden_t, q3, left_in, left, last = refs[-5:]
    base = (5 if step == 3 else 7) * CHIP
    for piece, row in zip(pieces, rows_of_step(step, place[1])):
        last[pl.ds(pl.multiple_of(row - base, TOK), TOK), :] = piece[...]
    g = fold(dot(q3[...], last[...], 1, 1), 3)
    g = jnp.concatenate(split(g, 2), axis=0)
    here = hidden_t[:, base : base + last.shape[0]]
    left[...] = left_in[...] + fold(dot(g, here, 1, 1), 2)


def left_call(step, place, pieces, hidden_t, q3, left_in):
    rows = TOK * len(pieces)
    return pl.pallas_call(
        functools.partial(left_kernel, step),
        in_specs=[SMEM] + [WHOLE] * (len(pieces) + 3),
        out_specs=[WHOLE] * 2,
        out_shape=[
            jax.ShapeDtypeStruct((RANK, UNITS), F32),
            kept((rows, D), BF),
        ],
        compiler_params=params(12),
        cost_estimate=SHORT,
        name="left_of_step",
    )(place, *map(held, pieces), held(hidden_t), held(q3), left_in)


def right_kernel(l0, l1, l2, l3, hidden_t, last_a, last_b, merged, p_out, right):
    left = ((l0[...] + l2[...]) + (l1[...] + l3[...])) * (1.0 / DP)
    rest = dot(left, left, 1, 1, HI)
    rows = lax.broadcasted_iota(jnp.int32, (RANK, RANK), 0)
    inverse = (rows == lax.broadcasted_iota(jnp.int32, (RANK, RANK), 1)).astype(F32)
    for k in range(RANK):
        scale = lax.rsqrt(rest[k : k + 1, k : k + 1])
        column = jnp.where(rows[:, 0:1] > k, rest[:, k : k + 1] * scale, 0.0)
        rest_row = rest[k : k + 1, :] * scale
        inverse_row = inverse[k : k + 1, :] * scale
        rest = rest - column * rest_row
        inverse = jnp.where(rows == k, inverse_row, inverse - column * inverse_row)
    factor = dot(inverse, left, 1, 0, HI)
    p_out[...] = factor
    high, low = split(factor, 2)
    p2 = jnp.concatenate([high, low], axis=0)
    mine = fold(dot(p2, hidden_t[:, EARLY:], 1, 0), 2)
    h2 = jnp.concatenate(split(mine, 2), axis=0)
    for i in range(NBLK):
        c = slice(i * BLK, (i + 1) * BLK)
        total = dot(p2, merged[:, c], 1, 0)
        total += dot(h2[:, : 2 * CHIP], last_a[:, c], 1, 0)
        total += dot(h2[:, 2 * CHIP :], last_b[:, c], 1, 0)
        right[:, :, c] = fold(total, 2).astype(BF).reshape(DP, RANK // DP, BLK)


def right_call(lefts, hidden_t, last_a, last_b, merged):
    return pl.pallas_call(
        right_kernel,
        in_specs=[WHOLE] * 8,
        out_specs=[WHOLE] * 2,
        out_shape=[
            jax.ShapeDtypeStruct((RANK, UNITS), F32),
            jax.ShapeDtypeStruct((DP, RANK // DP, D), BF),
        ],
        compiler_params=params(14),
        cost_estimate=cost(10**8, 8_000_000),
        name="right_factor",
    )(*lefts, held(hidden_t), held(last_a), held(last_b), held(merged))


def sum_kernel(parts, out):
    total = jnp.sum(parts[...].astype(F32), axis=0, keepdims=True)
    out[...] = jnp.broadcast_to(total.astype(BF), out.shape)


def sum_call(parts):
    return pl.pallas_call(
        sum_kernel,
        in_specs=[WHOLE],
        out_specs=WHOLE,
        out_shape=jax.ShapeDtypeStruct(parts.shape, BF),
        compiler_params=params(8),
        cost_estimate=cost(10**6, 500_000),
        name="sum_of_ranks",
    )(parts)


HALF = D // 2
WIDE = HALF // 2


def merge_kernel(hidden_t, last_a, last_b, merged, total):
    part = merged[...].astype(F32)
    part += dot(hidden_t[:, EARLY : EARLY + 2 * CHIP], last_a[...], 1, 0)
    part += dot(hidden_t[:, EARLY + 2 * CHIP :], last_b[...], 1, 0)
    total[...] = part.astype(BF)


def merge_call(half, hidden_t, last_a, last_b, merged):
    first = half * (HALF // WIDE)
    cols = lambda rows: pl.BlockSpec((rows, WIDE), lambda i: (0, first + i))
    return pl.pallas_call(
        merge_kernel,
        grid=(HALF // WIDE,),
        in_specs=[
            pl.BlockSpec((UNITS, ROWS), lambda i: (0, 0)),
            cols(2 * CHIP),
            cols(CHIP),
            cols(UNITS),
        ],
        out_specs=pl.BlockSpec((UNITS, WIDE), lambda i: (0, i)),
        out_shape=kept((UNITS, HALF), BF),
        compiler_params=params(14),
        cost_estimate=cost(3 * CHIP * UNITS * D, 6_000_000),
        name="weight_grad_rest",
    )(*map(from_hbm, (hidden_t, last_a, last_b, merged)))


def error_kernel(factor, lower, upper, summed, out, q, p2_t):
    i = pl.program_id(0)

    @pl.when(i == 0)
    def _():
        p2_t[...] = jnp.concatenate(split(jnp.transpose(factor[...]), 2), axis=1)

    mean = summed[...].astype(F32).reshape(RANK, WIDE) * (1.0 / DP)
    q[...] = mean
    rounded = mean.astype(BF)
    rounded = jnp.concatenate([rounded, rounded], axis=0)
    estimate = dot(p2_t[...], rounded, 1, 0)

    per = HALF // WIDE
    for k in range(2 * per):

        @pl.when(i == k)
        def _():
            part = (lower, upper)[k // per][:, k % per * WIDE : (k % per + 1) * WIDE]
            out[...] = (part.astype(F32) - estimate).astype(BF)


def error_call(factor, lower, upper, summed):
    cols = lambda rows: pl.BlockSpec((rows, WIDE), lambda i: (0, i))
    return pl.pallas_call(
        error_kernel,
        grid=(D // WIDE,),
        in_specs=[
            pl.BlockSpec((RANK, UNITS), lambda i: (0, 0)),
            WHOLE,
            WHOLE,
            pl.BlockSpec((DP, RANK // DP, WIDE), lambda i: (0, 0, i)),
        ],
        out_specs=[cols(UNITS), cols(RANK)],
        scratch_shapes=[pltpu.VMEM((UNITS, 2 * RANK), BF)],
        out_shape=[
            jax.ShapeDtypeStruct((UNITS, D), BF),
            jax.ShapeDtypeStruct((RANK, D), F32),
        ],
        compiler_params=params(8),
        cost_estimate=cost(2 * 64 * UNITS * D, 8_000_000),
        name="new_error",
    )(factor, held(lower), held(upper), summed)


def slots_of_step(s):
    return {0: [0], 4: [7]}.get(s, [2 * s - 1, 2 * s])


def finish_pre(grad, pre, stage):
    value, slope = gelu_pair(pre[0].astype(F32))
    stage[0] = (grad * pre[1].astype(F32) * slope).astype(BF)
    stage[1] = (grad * value).astype(BF)


def pre_kernel(s, place, *refs):
    slots = slots_of_step(s)
    count = 2 * len(slots) if s < 3 else 1
    pieces, refs = refs[:count], refs[count:]
    pres, refs = refs[: len(slots)], refs[len(slots) :]
    weight, (out, tokens, stage, sems) = refs[0], refs[-4:]
    if s < 3:
        for piece, row in zip(pieces, rows_of_step(s, place[1])):
            row = pl.multiple_of(row - slots[0] * CHIP, TOK)
            tokens[pl.ds(row, TOK), :] = piece[...]
        here = tokens[...]
    else:
        here = pieces[0][...]
    grad = dot(here, weight[...], 1, 1)
    copies = []
    for k, slot in enumerate(slots):
        finish_pre(grad[k * CHIP : (k + 1) * CHIP], pres[k], stage.at[k])
        row = pl.multiple_of(chip_of(slot, place[0]) * CHIP, CHIP)
        copies.append(
            pltpu.make_async_copy(stage.at[k], out.at[:, pl.ds(row, CHIP), :], sems.at[k])
        )
        copies[-1].start()
    for copy in copies:
        copy.wait()


def pre_call(s, place, pieces, pre, weight, so_far=None):
    slots = slots_of_step(s)
    chip = lambda slot: pl.BlockSpec((2, CHIP, UNITS), lambda i, p: (0, chip_of(slot, p[0]), 0))
    any_space = pl.BlockSpec(memory_space=pl.ANY)
    specs = [WHOLE] * len(pieces) + [chip(k) for k in slots] + [WHOLE]
    args = [place, *map(held, pieces), *([pre] * len(slots)), held(weight)]
    aliases = {}
    if so_far is not None:
        aliases = {len(args): 0}
        specs.append(any_space)
        args.append(so_far)
    rows = CHIP * len(slots)
    return pl.pallas_call(
        functools.partial(pre_kernel, s),
        grid_spec=pltpu.PrefetchScalarGridSpec(
            num_scalar_prefetch=1,
            grid=(1,),
            in_specs=specs,
            out_specs=any_space,
            scratch_shapes=[
                pltpu.VMEM((rows, D), BF),
                pltpu.VMEM((len(slots), 2, CHIP, UNITS), BF),
                pltpu.SemaphoreType.DMA((len(slots),)),
            ],
        ),
        out_shape=jax.ShapeDtypeStruct((2, ROWS, UNITS), BF),
        input_output_aliases=aliases,
        compiler_params=params(10),
        cost_estimate=SHORT,
        name="grad_pre",
    )(*args)


def on_device(grad_out, pre_act, down_weight, error, q_start):
    index = lax.axis_index("tensor").astype(jnp.int32)
    place = jnp.stack([index >> 1, index & 1])
    hidden_t = hidden_call(place, pre_act)
    q3 = jnp.concatenate(split_exactly(q_start, 3), axis=0)

    def pre_of(step, pieces, so_far=None):
        return pre_call(step, place, pieces, pre_act, down_weight, so_far)

    a0, b0 = grad_out, other_core(grad_out)
    a1, b1 = along_z(a0), along_z(after(b0, hidden_t))
    grad_pre = pre_of(0, [a0, b0])
    a2 = along_z(after(a1, grad_pre))
    b2 = along_z(after(b1, a1))
    xa1, xb1 = other_core(after(a1, b1)), other_core(after(b1, a1))
    a3 = along_z(after(a2, b1))
    xb1 = after(xb1, a2)
    grad_pre = pre_of(1, [a1, b1, xa1, xb1], grad_pre)
    b3 = along_z(after(b2, a2, grad_pre))
    xa2, xb2 = other_core(after(a2, b2, grad_pre)), other_core(after(b2, a2, grad_pre))
    a4 = along_z(after(a3, b2))
    grad_pre = pre_of(2, [a2, b2, xa2, xb2], grad_pre)
    xa2, xb2, _ = lax.optimization_barrier((xa2, xb2, a3))
    early = [a0, b0, a1, b1, xa1, xb1, a2, b2, xa2, xb2]
    merged, left = main_call(place, early, hidden_t, error, q3)
    xa3, xb3 = other_core(after(a3, b3, left)), other_core(after(b3, a3, left))
    xa4 = other_core(after(a4, b3, left))
    left, last_a = left_call(3, place, [a3, b3, xa3, xb3], hidden_t, q3, left)
    left, last_b = left_call(4, place, [a4, xa4], hidden_t, q3, left)

    grad_pre = pre_of(3, [after(last_a, left)], grad_pre)
    lefts = sum_over_ring(left, 0)
    left = sum_of_four(lefts[0], lefts[1], lefts[2], after(lefts[3], grad_pre))
    grad_pre = pre_of(4, [after(last_b, left)], grad_pre)
    lefts = sum_over_ring(left, 1)
    lefts[3] = after(lefts[3], grad_pre)
    p_factor, right = right_call(lefts, hidden_t, last_a, last_b, merged)

    parts = lax.all_to_all(right, "dp", 0, 0, tiled=True)
    lower = merge_call(0, after(hidden_t, right), last_a, last_b, merged)
    summed = sum_call(after(parts, lower))
    right = lax.all_to_all(summed, "dp", 0, 0, tiled=True)
    upper = merge_call(1, after(hidden_t, summed), last_a, last_b, merged)
    new_error, q_factor = error_call(p_factor, lower, upper, right)
    return (grad_pre, new_error, p_factor, q_factor)


def solution(mesh):
    placed = (
        P(("dp", "tensor"), None),
        P(None, "dp", "tensor"),
        P("tensor", None),
        P(("dp", "tensor"), None),
        P("tensor", None),
    )
    return jax.shard_map(
        on_device,
        mesh=mesh,
        in_specs=placed,
        out_specs=(
            P(None, "dp", "tensor"),
            P(("dp", "tensor"), None),
            P(None, "tensor"),
            P("tensor", None),
        ),
        check_vma=False,
    )
```

```python
import functools

import jax
import jax.numpy as jnp
from jax import lax
from jax.experimental import pallas as pl
from jax.experimental.pallas import tpu as pltpu
from jax.sharding import PartitionSpec as P

BF = jnp.bfloat16
F32 = jnp.float32
HI = lax.Precision.HIGHEST
DP = 16
NZ = 8
TOK = 64
CHIP = 2 * TOK
D = 3584
UNITS = 512
ROWS = 1024
EARLY = 5 * CHIP
RANK = 32
BLK = 512
NBLK = D // BLK
MIB = 1024 * 1024


def gelu_pair(value):
    coeff = 0.7978845608028654
    tanh_val = jnp.tanh(coeff * (value + 0.044715 * value * value * value))
    gelu_value = 0.5 * value * (1.0 + tanh_val)
    gelu_slope = 0.5 * (1.0 + tanh_val) + 0.5 * value * (1.0 - tanh_val * tanh_val) * coeff * (
        1.0 + 3.0 * 0.044715 * value * value
    )
    return (gelu_value, gelu_slope)


def split(value, terms):
    parts = []
    for _ in range(terms):
        part = value.astype(BF)
        parts.append(part)
        value = value - part.astype(F32)
    return parts


def split_exactly(value, terms):
    parts = []
    for _ in range(terms):
        part = lax.reduce_precision(value, 8, 7)
        parts.append(part.astype(BF))
        value = value - part
    return parts


def dot(a, b, ca, cb, precision=None):
    return lax.dot_general(
        a, b, (((ca,), (cb,)), ((), ())), preferred_element_type=F32, precision=precision
    )


def fold(stacked, terms):
    total = stacked[0:RANK]
    for k in range(1, terms):
        total = total + stacked[k * RANK : (k + 1) * RANK]
    return total


def chip_of(slot, z):
    return lax.rem(z + jnp.where(slot % 2 == 1, 2 * NZ - (slot + 1) // 2, NZ + slot // 2), NZ)


def rows_of_step(s, core):
    if s == 0:
        return [core * TOK, (1 - core) * TOK]
    if s == 4:
        return [(14 + core) * TOK, (15 - core) * TOK]
    return [
        (4 * s - 2 + 3 * core) * TOK,
        (4 * s - 1 + core) * TOK,
        (4 * s + 1 - 3 * core) * TOK,
        (4 * s - core) * TOK,
    ]


def after(value, *others):
    return lax.optimization_barrier((value,) + others)[0]


def other_core(value):
    return lax.ppermute(value, "tensor", [(i, i ^ 1) for i in range(2 * NZ)])


def along_z(value):
    return lax.ppermute(
        value, "tensor", [(i, (i + 2 - 4 * (i % 2)) % (2 * NZ)) for i in range(2 * NZ)]
    )


def sum_over_ring(value, turn):
    def pairs(k):
        for i in range(DP * 2 * NZ):
            dp, t = divmod(i, 2 * NZ)
            x, y = divmod(dp, 4)
            if (t + turn) % 2 == 0:
                x = (x + k) % 4
            else:
                y = (y + k) % 4
            yield (i, (4 * x + y) * 2 * NZ + t)

    return [value] + [lax.ppermute(value, ("dp", "tensor"), list(pairs(k))) for k in (1, 2, 3)]


def sum_of_four(a, b, c, d):
    return (a + c) + (b + d)


SMEM = pl.BlockSpec(memory_space=pltpu.SMEM)
WHOLE = pl.BlockSpec(memory_space=pltpu.VMEM)


def kept(shape, dtype):
    return pltpu.VMEM(shape, dtype)


def held(value):
    return pltpu.with_memory_space_constraint(value, pltpu.VMEM)


def kept_out(shape, dtype):
    return pltpu.HBM(shape, dtype)


def from_hbm(value):
    return pltpu.with_memory_space_constraint(value, pltpu.HBM)


def params(mib):
    return pltpu.CompilerParams(vmem_limit_bytes=mib * MIB)


def cost(flops, moved):
    return pl.CostEstimate(flops=flops, bytes_accessed=moved, transcendentals=0)


SHORT = cost(10**6, 10**5)


def hidden_kernel(place, pre, hidden_t):
    value, _ = gelu_pair(pre[0].astype(F32))
    hidden = (value * pre[1].astype(F32)).astype(BF).astype(F32)
    hidden_t[...] = jnp.transpose(hidden).astype(BF)


def hidden_call(place, pre):
    return pl.pallas_call(
        hidden_kernel,
        grid_spec=pltpu.PrefetchScalarGridSpec(
            num_scalar_prefetch=1,
            grid=(NZ,),
            in_specs=[pl.BlockSpec((2, CHIP, UNITS), lambda i, p: (0, chip_of(i, p[0]), 0))],
            out_specs=pl.BlockSpec((UNITS, CHIP), lambda i, p: (0, i)),
        ),
        out_shape=kept((UNITS, ROWS), BF),
        compiler_params=params(8),
        cost_estimate=SHORT,
        name="hidden",
    )(place, pre)


def main_kernel(place, *refs):
    pieces = refs[:10]
    hidden_t, error, q3, merged, left, tokens, g_acc, e_acc = refs[10:]
    i = pl.program_id(0)
    rows = [r for s in range(3) for r in rows_of_step(s, place[1])]
    for piece, row in zip(pieces, rows):
        tokens[pl.ds(pl.multiple_of(row, TOK), TOK), :] = piece[...]

    @pl.when(i == 0)
    def _():
        g_acc[...] = jnp.zeros_like(g_acc)
        e_acc[...] = jnp.zeros_like(e_acc)

    block = tokens[...]
    err = error[...]
    merged[...] = (dot(hidden_t[:, :EARLY], block, 1, 0) + err.astype(F32)).astype(BF)
    q = q3[...]
    g_acc[...] += dot(q, block, 1, 1)
    e_acc[...] += dot(q, err, 1, 1)

    @pl.when(i == NBLK - 1)
    def _():
        g = jnp.concatenate(split(fold(g_acc[...], 3), 2), axis=0)
        left[...] = fold(e_acc[...], 3) + fold(dot(g, hidden_t[:, :EARLY], 1, 1), 2)


def main_call(place, pieces, hidden_t, error, q3):
    whole = lambda shape: pl.BlockSpec(shape, lambda i, p: (0, 0))
    cols = lambda rows: pl.BlockSpec((rows, BLK), lambda i, p: (0, i))
    return pl.pallas_call(
        main_kernel,
        grid_spec=pltpu.PrefetchScalarGridSpec(
            num_scalar_prefetch=1,
            grid=(NBLK,),
            in_specs=[cols(TOK)] * 10
            + [whole((UNITS, ROWS)), cols(UNITS), cols(3 * RANK)],
            out_specs=[cols(UNITS), whole((RANK, UNITS))],
            scratch_shapes=[
                pltpu.VMEM((EARLY, BLK), BF),
                pltpu.VMEM((3 * RANK, EARLY), F32),
                pltpu.VMEM((3 * RANK, UNITS), F32),
            ],
        ),
        out_shape=[
            kept((UNITS, D), BF),
            jax.ShapeDtypeStruct((RANK, UNITS), F32),
        ],
        compiler_params=params(14),
        cost_estimate=SHORT,
        name="weight_grad",
    )(place, *map(held, pieces), held(hidden_t), error, q3)


def left_kernel(step, place, *refs):
    pieces = refs[:-5]
    hidden_t, q3, left_in, left, last = refs[-5:]
    base = (5 if step == 3 else 7) * CHIP
    for piece, row in zip(pieces, rows_of_step(step, place[1])):
        last[pl.ds(pl.multiple_of(row - base, TOK), TOK), :] = piece[...]
    g = fold(dot(q3[...], last[...], 1, 1), 3)
    g = jnp.concatenate(split(g, 2), axis=0)
    here = hidden_t[:, base : base + last.shape[0]]
    left[...] = left_in[...] + fold(dot(g, here, 1, 1), 2)


def left_call(step, place, pieces, hidden_t, q3, left_in):
    rows = TOK * len(pieces)
    return pl.pallas_call(
        functools.partial(left_kernel, step),
        in_specs=[SMEM] + [WHOLE] * (len(pieces) + 3),
        out_specs=[WHOLE] * 2,
        out_shape=[
            jax.ShapeDtypeStruct((RANK, UNITS), F32),
            kept((rows, D), BF),
        ],
        compiler_params=params(12),
        cost_estimate=SHORT,
        name="left_of_step",
    )(place, *map(held, pieces), held(hidden_t), held(q3), left_in)


def right_kernel(l0, l1, l2, l3, hidden_t, last_a, last_b, merged, p_out, right):
    left = ((l0[...] + l2[...]) + (l1[...] + l3[...])) * (1.0 / DP)
    rest = dot(left, left, 1, 1, HI)
    rows = lax.broadcasted_iota(jnp.int32, (RANK, RANK), 0)
    inverse = (rows == lax.broadcasted_iota(jnp.int32, (RANK, RANK), 1)).astype(F32)
    for k in range(RANK):
        scale = lax.rsqrt(rest[k : k + 1, k : k + 1])
        column = jnp.where(rows[:, 0:1] > k, rest[:, k : k + 1] * scale, 0.0)
        rest_row = rest[k : k + 1, :] * scale
        inverse_row = inverse[k : k + 1, :] * scale
        rest = rest - column * rest_row
        inverse = jnp.where(rows == k, inverse_row, inverse - column * inverse_row)
    factor = dot(inverse, left, 1, 0, HI)
    p_out[...] = factor
    high, low = split(factor, 2)
    p2 = jnp.concatenate([high, low], axis=0)
    mine = fold(dot(p2, hidden_t[:, EARLY:], 1, 0), 2)
    h2 = jnp.concatenate(split(mine, 2), axis=0)
    for i in range(NBLK):
        c = slice(i * BLK, (i + 1) * BLK)
        total = dot(p2, merged[:, c], 1, 0)
        total += dot(h2[:, : 2 * CHIP], last_a[:, c], 1, 0)
        total += dot(h2[:, 2 * CHIP :], last_b[:, c], 1, 0)
        right[:, :, c] = fold(total, 2).astype(BF).reshape(DP, RANK // DP, BLK)


def right_call(lefts, hidden_t, last_a, last_b, merged):
    return pl.pallas_call(
        right_kernel,
        in_specs=[WHOLE] * 8,
        out_specs=[WHOLE] * 2,
        out_shape=[
            jax.ShapeDtypeStruct((RANK, UNITS), F32),
            jax.ShapeDtypeStruct((DP, RANK // DP, D), BF),
        ],
        compiler_params=params(14),
        cost_estimate=cost(10**8, 8_000_000),
        name="right_factor",
    )(*lefts, held(hidden_t), held(last_a), held(last_b), held(merged))


def sum_kernel(parts, out):
    total = jnp.sum(parts[...].astype(F32), axis=0, keepdims=True)
    out[...] = jnp.broadcast_to(total.astype(BF), out.shape)


def sum_call(parts):
    return pl.pallas_call(
        sum_kernel,
        in_specs=[WHOLE],
        out_specs=WHOLE,
        out_shape=jax.ShapeDtypeStruct(parts.shape, BF),
        compiler_params=params(8),
        cost_estimate=cost(10**6, 500_000),
        name="sum_of_ranks",
    )(parts)


HALF = D // 2
WIDE = HALF // 2


def merge_kernel(hidden_t, last_a, last_b, merged, total):
    part = merged[...].astype(F32)
    part += dot(hidden_t[:, EARLY : EARLY + 2 * CHIP], last_a[...], 1, 0)
    part += dot(hidden_t[:, EARLY + 2 * CHIP :], last_b[...], 1, 0)
    total[...] = part.astype(BF)


def merge_call(half, hidden_t, last_a, last_b, merged):
    first = half * (HALF // WIDE)
    cols = lambda rows: pl.BlockSpec((rows, WIDE), lambda i: (0, first + i))
    return pl.pallas_call(
        merge_kernel,
        grid=(HALF // WIDE,),
        in_specs=[
            pl.BlockSpec((UNITS, ROWS), lambda i: (0, 0)),
            cols(2 * CHIP),
            cols(CHIP),
            cols(UNITS),
        ],
        out_specs=pl.BlockSpec((UNITS, WIDE), lambda i: (0, i)),
        out_shape=kept((UNITS, HALF), BF),
        compiler_params=params(14),
        cost_estimate=cost(3 * CHIP * UNITS * D, 6_000_000),
        name="weight_grad_rest",
    )(*map(from_hbm, (hidden_t, last_a, last_b, merged)))


def error_kernel(factor, lower, upper, summed, out, q, p2_t):
    i = pl.program_id(0)

    @pl.when(i == 0)
    def _():
        p2_t[...] = jnp.concatenate(split(jnp.transpose(factor[...]), 2), axis=1)

    mean = summed[...].astype(F32).reshape(RANK, WIDE) * (1.0 / DP)
    q[...] = mean
    rounded = mean.astype(BF)
    rounded = jnp.concatenate([rounded, rounded], axis=0)
    estimate = dot(p2_t[...], rounded, 1, 0)

    per = HALF // WIDE
    for k in range(2 * per):

        @pl.when(i == k)
        def _():
            part = (lower, upper)[k // per][:, k % per * WIDE : (k % per + 1) * WIDE]
            out[...] = (part.astype(F32) - estimate).astype(BF)


def error_call(factor, lower, upper, summed):
    cols = lambda rows: pl.BlockSpec((rows, WIDE), lambda i: (0, i))
    return pl.pallas_call(
        error_kernel,
        grid=(D // WIDE,),
        in_specs=[
            pl.BlockSpec((RANK, UNITS), lambda i: (0, 0)),
            WHOLE,
            WHOLE,
            pl.BlockSpec((DP, RANK // DP, WIDE), lambda i: (0, 0, i)),
        ],
        out_specs=[cols(UNITS), cols(RANK)],
        scratch_shapes=[pltpu.VMEM((UNITS, 2 * RANK), BF)],
        out_shape=[
            jax.ShapeDtypeStruct((UNITS, D), BF),
            jax.ShapeDtypeStruct((RANK, D), F32),
        ],
        compiler_params=params(8),
        cost_estimate=cost(2 * 64 * UNITS * D, 8_000_000),
        name="new_error",
    )(factor, held(lower), held(upper), summed)


def slots_of_step(s):
    return {0: [0], 3: [5, 6, 7]}.get(s, [2 * s - 1, 2 * s])


def finish_pre(grad, pre, stage):
    value, slope = gelu_pair(pre[0].astype(F32))
    stage[0] = (grad * pre[1].astype(F32) * slope).astype(BF)
    stage[1] = (grad * value).astype(BF)


def pre_kernel(s, place, *refs):
    slots = slots_of_step(s)
    count = 2 if s == 3 else 2 * len(slots)
    pieces, refs = refs[:count], refs[count:]
    pres, refs = refs[: len(slots)], refs[len(slots) :]
    weight, (out, tokens, stage, sems) = refs[0], refs[-4:]
    if s < 3:
        for piece, row in zip(pieces, rows_of_step(s, place[1])):
            row = pl.multiple_of(row - slots[0] * CHIP, TOK)
            tokens[pl.ds(row, TOK), :] = piece[...]
        grad = dot(tokens[...], weight[...], 1, 1)
    else:
        grad = jnp.concatenate([dot(here[...], weight[...], 1, 1) for here in pieces], axis=0)
    copies = []
    for k, slot in enumerate(slots):
        finish_pre(grad[k * CHIP : (k + 1) * CHIP], pres[k], stage.at[k])
        row = pl.multiple_of(chip_of(slot, place[0]) * CHIP, CHIP)
        copies.append(
            pltpu.make_async_copy(stage.at[k], out.at[:, pl.ds(row, CHIP), :], sems.at[k])
        )
        copies[-1].start()
    for copy in copies:
        copy.wait()


def pre_call(s, place, pieces, pre, weight, so_far=None):
    slots = slots_of_step(s)
    chip = lambda slot: pl.BlockSpec((2, CHIP, UNITS), lambda i, p: (0, chip_of(slot, p[0]), 0))
    any_space = pl.BlockSpec(memory_space=pl.ANY)
    specs = [WHOLE] * len(pieces) + [chip(k) for k in slots] + [WHOLE]
    args = [place, *map(held, pieces), *([pre] * len(slots)), held(weight)]
    aliases = {}
    if so_far is not None:
        aliases = {len(args): 0}
        specs.append(any_space)
        args.append(so_far)
    rows = CHIP * len(slots)
    return pl.pallas_call(
        functools.partial(pre_kernel, s),
        grid_spec=pltpu.PrefetchScalarGridSpec(
            num_scalar_prefetch=1,
            grid=(1,),
            in_specs=specs,
            out_specs=any_space,
            scratch_shapes=[
                pltpu.VMEM((rows, D), BF),
                pltpu.VMEM((len(slots), 2, CHIP, UNITS), BF),
                pltpu.SemaphoreType.DMA((len(slots),)),
            ],
        ),
        out_shape=jax.ShapeDtypeStruct((2, ROWS, UNITS), BF),
        input_output_aliases=aliases,
        compiler_params=params(14),
        cost_estimate=SHORT,
        name="grad_pre",
    )(*args)


def on_device(grad_out, pre_act, down_weight, error, q_start):
    index = lax.axis_index("tensor").astype(jnp.int32)
    place = jnp.stack([index >> 1, index & 1])
    hidden_t = hidden_call(place, pre_act)
    q3 = jnp.concatenate(split_exactly(q_start, 3), axis=0)

    def pre_of(step, pieces, so_far=None):
        return pre_call(step, place, pieces, pre_act, down_weight, so_far)

    a0, b0 = grad_out, other_core(grad_out)
    a1, b1 = along_z(a0), along_z(after(b0, hidden_t))
    grad_pre = pre_of(0, [a0, b0])
    a2 = along_z(after(a1, grad_pre))
    b2 = along_z(after(b1, a1))
    xa1, xb1 = other_core(after(a1, b1)), other_core(after(b1, a1))
    a3 = along_z(after(a2, b1))
    xb1 = after(xb1, a2)
    grad_pre = pre_of(1, [a1, b1, xa1, xb1], grad_pre)
    b3 = along_z(after(b2, a2, grad_pre))
    xa2, xb2 = other_core(after(a2, b2, grad_pre)), other_core(after(b2, a2, grad_pre))
    a4 = along_z(after(a3, b2))
    grad_pre = pre_of(2, [a2, b2, xa2, xb2], grad_pre)
    xa2, xb2, _ = lax.optimization_barrier((xa2, xb2, a3))
    early = [a0, b0, a1, b1, xa1, xb1, a2, b2, xa2, xb2]
    merged, left = main_call(place, early, hidden_t, error, q3)
    xa3, xb3 = other_core(after(a3, b3, left)), other_core(after(b3, a3, left))
    xa4 = other_core(after(a4, b3, left))
    left, last_a = left_call(3, place, [a3, b3, xa3, xb3], hidden_t, q3, left)
    left, last_b = left_call(4, place, [a4, xa4], hidden_t, q3, left)

    lefts = sum_over_ring(left, 0)
    left = sum_of_four(lefts[0], lefts[1], lefts[2], after(lefts[3], grad_pre))
    grad_pre = pre_of(3, [after(last_a, left), last_b], grad_pre)
    lefts = sum_over_ring(left, 1)
    lefts[3] = after(lefts[3], grad_pre)
    p_factor, right = right_call(lefts, hidden_t, last_a, last_b, merged)

    parts = lax.all_to_all(right, "dp", 0, 0, tiled=True)
    lower = merge_call(0, after(hidden_t, right), last_a, last_b, merged)
    summed = sum_call(after(parts, lower))
    right = lax.all_to_all(summed, "dp", 0, 0, tiled=True)
    upper = merge_call(1, after(hidden_t, summed), last_a, last_b, merged)
    new_error, q_factor = error_call(p_factor, lower, upper, right)
    return (grad_pre, new_error, p_factor, q_factor)


def solution(mesh):
    placed = (
        P(("dp", "tensor"), None),
        P(None, "dp", "tensor"),
        P("tensor", None),
        P(("dp", "tensor"), None),
        P("tensor", None),
    )
    return jax.shard_map(
        on_device,
        mesh=mesh,
        in_specs=placed,
        out_specs=(
            P(None, "dp", "tensor"),
            P(("dp", "tensor"), None),
            P(None, "tensor"),
            P("tensor", None),
        ),
        check_vma=False,
    )
```

```python
import functools

import jax
import jax.numpy as jnp
from jax import lax
from jax.experimental import pallas as pl
from jax.experimental.pallas import tpu as pltpu
from jax.sharding import PartitionSpec as P

BF = jnp.bfloat16
F32 = jnp.float32
HI = lax.Precision.HIGHEST
DP = 16
NZ = 8
TOK = 64
CHIP = 2 * TOK
D = 3584
UNITS = 512
ROWS = 1024
EARLY = 5 * CHIP
RANK = 32
BLK = 512
NBLK = D // BLK
MIB = 1024 * 1024


def gelu_pair(value):
    coeff = 0.7978845608028654
    tanh_val = jnp.tanh(coeff * (value + 0.044715 * value * value * value))
    gelu_value = 0.5 * value * (1.0 + tanh_val)
    gelu_slope = 0.5 * (1.0 + tanh_val) + 0.5 * value * (1.0 - tanh_val * tanh_val) * coeff * (
        1.0 + 3.0 * 0.044715 * value * value
    )
    return (gelu_value, gelu_slope)


def split(value, terms):
    parts = []
    for _ in range(terms):
        part = value.astype(BF)
        parts.append(part)
        value = value - part.astype(F32)
    return parts


def split_exactly(value, terms):
    parts = []
    for _ in range(terms):
        part = lax.reduce_precision(value, 8, 7)
        parts.append(part.astype(BF))
        value = value - part
    return parts


def dot(a, b, ca, cb, precision=None):
    return lax.dot_general(
        a, b, (((ca,), (cb,)), ((), ())), preferred_element_type=F32, precision=precision
    )


def fold(stacked, terms):
    total = stacked[0:RANK]
    for k in range(1, terms):
        total = total + stacked[k * RANK : (k + 1) * RANK]
    return total


def chip_of(slot, z):
    return lax.rem(z + jnp.where(slot % 2 == 1, 2 * NZ - (slot + 1) // 2, NZ + slot // 2), NZ)


def rows_of_step(s, core):
    if s == 0:
        return [core * TOK, (1 - core) * TOK]
    if s == 4:
        return [(14 + core) * TOK, (15 - core) * TOK]
    return [
        (4 * s - 2 + 3 * core) * TOK,
        (4 * s - 1 + core) * TOK,
        (4 * s + 1 - 3 * core) * TOK,
        (4 * s - core) * TOK,
    ]


def after(value, *others):
    return lax.optimization_barrier((value,) + others)[0]


def other_core(value):
    return lax.ppermute(value, "tensor", [(i, i ^ 1) for i in range(2 * NZ)])


def along_z(value):
    return lax.ppermute(
        value, "tensor", [(i, (i + 2 - 4 * (i % 2)) % (2 * NZ)) for i in range(2 * NZ)]
    )


def sum_over_ring(value, turn):
    def pairs(k):
        for i in range(DP * 2 * NZ):
            dp, t = divmod(i, 2 * NZ)
            x, y = divmod(dp, 4)
            if (t + turn) % 2 == 0:
                x = (x + k) % 4
            else:
                y = (y + k) % 4
            yield (i, (4 * x + y) * 2 * NZ + t)

    return [value] + [lax.ppermute(value, ("dp", "tensor"), list(pairs(k))) for k in (1, 2, 3)]


def sum_of_four(a, b, c, d):
    return (a + c) + (b + d)


SMEM = pl.BlockSpec(memory_space=pltpu.SMEM)
WHOLE = pl.BlockSpec(memory_space=pltpu.VMEM)


def kept(shape, dtype):
    return pltpu.VMEM(shape, dtype)


def held(value):
    return pltpu.with_memory_space_constraint(value, pltpu.VMEM)


def kept_out(shape, dtype):
    return pltpu.HBM(shape, dtype)


def from_hbm(value):
    return pltpu.with_memory_space_constraint(value, pltpu.HBM)


def params(mib):
    return pltpu.CompilerParams(vmem_limit_bytes=mib * MIB)


def cost(flops, moved):
    return pl.CostEstimate(flops=flops, bytes_accessed=moved, transcendentals=0)


SHORT = cost(10**6, 10**5)


def hidden_kernel(place, pre, hidden_t):
    value, _ = gelu_pair(pre[0].astype(F32))
    hidden = (value * pre[1].astype(F32)).astype(BF).astype(F32)
    hidden_t[...] = jnp.transpose(hidden).astype(BF)


def hidden_call(place, pre):
    return pl.pallas_call(
        hidden_kernel,
        grid_spec=pltpu.PrefetchScalarGridSpec(
            num_scalar_prefetch=1,
            grid=(NZ,),
            in_specs=[pl.BlockSpec((2, CHIP, UNITS), lambda i, p: (0, chip_of(i, p[0]), 0))],
            out_specs=pl.BlockSpec((UNITS, CHIP), lambda i, p: (0, i)),
        ),
        out_shape=kept((UNITS, ROWS), BF),
        compiler_params=params(8),
        cost_estimate=SHORT,
        name="hidden",
    )(place, pre)


def main_kernel(place, *refs):
    pieces = refs[:10]
    hidden_t, error, q3, merged, left, tokens, g_acc, e_acc = refs[10:]
    i = pl.program_id(0)
    rows = [r for s in range(3) for r in rows_of_step(s, place[1])]
    for piece, row in zip(pieces, rows):
        tokens[pl.ds(pl.multiple_of(row, TOK), TOK), :] = piece[...]

    @pl.when(i == 0)
    def _():
        g_acc[...] = jnp.zeros_like(g_acc)
        e_acc[...] = jnp.zeros_like(e_acc)

    block = tokens[...]
    err = error[...]
    merged[...] = (dot(hidden_t[:, :EARLY], block, 1, 0) + err.astype(F32)).astype(BF)
    q = q3[...]
    g_acc[...] += dot(q, block, 1, 1)
    e_acc[...] += dot(q, err, 1, 1)

    @pl.when(i == NBLK - 1)
    def _():
        g = jnp.concatenate(split(fold(g_acc[...], 3), 2), axis=0)
        left[...] = fold(e_acc[...], 3) + fold(dot(g, hidden_t[:, :EARLY], 1, 1), 2)


def main_call(place, pieces, hidden_t, error, q3):
    whole = lambda shape: pl.BlockSpec(shape, lambda i, p: (0, 0))
    cols = lambda rows: pl.BlockSpec((rows, BLK), lambda i, p: (0, i))
    return pl.pallas_call(
        main_kernel,
        grid_spec=pltpu.PrefetchScalarGridSpec(
            num_scalar_prefetch=1,
            grid=(NBLK,),
            in_specs=[cols(TOK)] * 10
            + [whole((UNITS, ROWS)), cols(UNITS), cols(3 * RANK)],
            out_specs=[cols(UNITS), whole((RANK, UNITS))],
            scratch_shapes=[
                pltpu.VMEM((EARLY, BLK), BF),
                pltpu.VMEM((3 * RANK, EARLY), F32),
                pltpu.VMEM((3 * RANK, UNITS), F32),
            ],
        ),
        out_shape=[
            kept((UNITS, D), BF),
            jax.ShapeDtypeStruct((RANK, UNITS), F32),
        ],
        compiler_params=params(14),
        cost_estimate=SHORT,
        name="weight_grad",
    )(place, *map(held, pieces), held(hidden_t), error, q3)


def left_kernel(step, place, *refs):
    pieces = refs[:-5]
    hidden_t, q3, left_in, left, last = refs[-5:]
    base = (5 if step == 3 else 7) * CHIP
    for piece, row in zip(pieces, rows_of_step(step, place[1])):
        last[pl.ds(pl.multiple_of(row - base, TOK), TOK), :] = piece[...]
    g = fold(dot(q3[...], last[...], 1, 1), 3)
    g = jnp.concatenate(split(g, 2), axis=0)
    here = hidden_t[:, base : base + last.shape[0]]
    left[...] = left_in[...] + fold(dot(g, here, 1, 1), 2)


def left_call(step, place, pieces, hidden_t, q3, left_in):
    rows = TOK * len(pieces)
    return pl.pallas_call(
        functools.partial(left_kernel, step),
        in_specs=[SMEM] + [WHOLE] * (len(pieces) + 3),
        out_specs=[WHOLE] * 2,
        out_shape=[
            jax.ShapeDtypeStruct((RANK, UNITS), F32),
            kept((rows, D), BF),
        ],
        compiler_params=params(12),
        cost_estimate=SHORT,
        name="left_of_step",
    )(place, *map(held, pieces), held(hidden_t), held(q3), left_in)


def right_kernel(l0, l1, l2, l3, hidden_t, last_a, last_b, merged, p_out, right):
    left = ((l0[...] + l2[...]) + (l1[...] + l3[...])) * (1.0 / DP)
    rest = dot(left, left, 1, 1, HI)
    rows = lax.broadcasted_iota(jnp.int32, (RANK, RANK), 0)
    inverse = (rows == lax.broadcasted_iota(jnp.int32, (RANK, RANK), 1)).astype(F32)
    for k in range(RANK):
        scale = lax.rsqrt(rest[k : k + 1, k : k + 1])
        column = jnp.where(rows[:, 0:1] > k, rest[:, k : k + 1] * scale, 0.0)
        rest_row = rest[k : k + 1, :] * scale
        inverse_row = inverse[k : k + 1, :] * scale
        rest = rest - column * rest_row
        inverse = jnp.where(rows == k, inverse_row, inverse - column * inverse_row)
    factor = dot(inverse, left, 1, 0, HI)
    p_out[...] = factor
    high, low = split(factor, 2)
    p2 = jnp.concatenate([high, low], axis=0)
    mine = fold(dot(p2, hidden_t[:, EARLY:], 1, 0), 2)
    h2 = jnp.concatenate(split(mine, 2), axis=0)
    for i in range(NBLK):
        c = slice(i * BLK, (i + 1) * BLK)
        total = dot(p2, merged[:, c], 1, 0)
        total += dot(h2[:, : 2 * CHIP], last_a[:, c], 1, 0)
        total += dot(h2[:, 2 * CHIP :], last_b[:, c], 1, 0)
        right[:, :, c] = fold(total, 2).astype(BF).reshape(DP, RANK // DP, BLK)


def right_call(lefts, hidden_t, last_a, last_b, merged):
    return pl.pallas_call(
        right_kernel,
        in_specs=[WHOLE] * 8,
        out_specs=[WHOLE] * 2,
        out_shape=[
            jax.ShapeDtypeStruct((RANK, UNITS), F32),
            jax.ShapeDtypeStruct((DP, RANK // DP, D), BF),
        ],
        compiler_params=params(14),
        cost_estimate=cost(10**8, 8_000_000),
        name="right_factor",
    )(*lefts, held(hidden_t), held(last_a), held(last_b), held(merged))


def sum_kernel(parts, out):
    total = jnp.sum(parts[...].astype(F32), axis=0, keepdims=True)
    out[...] = jnp.broadcast_to(total.astype(BF), out.shape)


def sum_call(parts):
    return pl.pallas_call(
        sum_kernel,
        in_specs=[WHOLE],
        out_specs=WHOLE,
        out_shape=jax.ShapeDtypeStruct(parts.shape, BF),
        compiler_params=params(8),
        cost_estimate=cost(10**6, 500_000),
        name="sum_of_ranks",
    )(parts)


HALF = D // 2
WIDE = HALF // 2


def merge_kernel(hidden_t, last_a, last_b, merged, total):
    part = merged[...].astype(F32)
    part += dot(hidden_t[:, EARLY : EARLY + 2 * CHIP], last_a[...], 1, 0)
    part += dot(hidden_t[:, EARLY + 2 * CHIP :], last_b[...], 1, 0)
    total[...] = part.astype(BF)


def merge_call(half, hidden_t, last_a, last_b, merged):
    place = kept if half else kept_out
    first = half * (HALF // WIDE)
    cols = lambda rows: pl.BlockSpec((rows, WIDE), lambda i: (0, first + i))
    return pl.pallas_call(
        merge_kernel,
        grid=(HALF // WIDE,),
        in_specs=[
            pl.BlockSpec((UNITS, ROWS), lambda i: (0, 0)),
            cols(2 * CHIP),
            cols(CHIP),
            cols(UNITS),
        ],
        out_specs=pl.BlockSpec((UNITS, WIDE), lambda i: (0, i)),
        out_shape=place((UNITS, HALF), BF),
        compiler_params=params(14),
        cost_estimate=cost(3 * CHIP * UNITS * D, 6_000_000),
        name="weight_grad_rest",
    )(*map(from_hbm, (hidden_t, last_a, last_b, merged)))


def error_kernel(factor, lower, upper, summed, out, q, p2_t, low, sem):
    i = pl.program_id(0)
    per = HALF // WIDE
    load = pltpu.make_async_copy(lower, low, sem)

    @pl.when(i == 0)
    def _():
        load.start()
        p2_t[...] = jnp.concatenate(split(jnp.transpose(factor[...]), 2), axis=1)

    mean = summed[...].astype(F32).reshape(RANK, WIDE) * (1.0 / DP)
    q[...] = mean
    rounded = mean.astype(BF)
    rounded = jnp.concatenate([rounded, rounded], axis=0)
    estimate = dot(p2_t[...], rounded, 1, 0)

    @pl.when(i == per)
    def _():
        load.wait()

    for k in range(2 * per):

        @pl.when(i == k)
        def _():
            part = (upper, low)[k // per][:, k % per * WIDE : (k % per + 1) * WIDE]
            out[...] = (part.astype(F32) - estimate).astype(BF)


def error_call(factor, lower, upper, summed):
    per = HALF // WIDE
    turned = lambda i: lax.rem(i + per, 2 * per)
    cols = lambda rows: pl.BlockSpec((rows, WIDE), lambda i: (0, turned(i)))
    return pl.pallas_call(
        error_kernel,
        grid=(D // WIDE,),
        in_specs=[
            pl.BlockSpec((RANK, UNITS), lambda i: (0, 0)),
            pl.BlockSpec(memory_space=pl.ANY),
            WHOLE,
            pl.BlockSpec((DP, RANK // DP, WIDE), lambda i: (0, 0, turned(i))),
        ],
        out_specs=[cols(UNITS), cols(RANK)],
        scratch_shapes=[
            pltpu.VMEM((UNITS, 2 * RANK), BF),
            pltpu.VMEM((UNITS, HALF), BF),
            pltpu.SemaphoreType.DMA,
        ],
        out_shape=[
            jax.ShapeDtypeStruct((UNITS, D), BF),
            jax.ShapeDtypeStruct((RANK, D), F32),
        ],
        compiler_params=params(10),
        cost_estimate=cost(2 * 64 * UNITS * D, 8_000_000),
        name="new_error",
    )(factor, from_hbm(lower), held(upper), summed)


def slots_of_step(s):
    return {0: [0], 3: [5, 6, 7]}.get(s, [2 * s - 1, 2 * s])


def finish_pre(grad, pre, stage):
    value, slope = gelu_pair(pre[0].astype(F32))
    stage[0] = (grad * pre[1].astype(F32) * slope).astype(BF)
    stage[1] = (grad * value).astype(BF)


def pre_kernel(s, place, *refs):
    slots = slots_of_step(s)
    count = 2 if s == 3 else 2 * len(slots)
    pieces, refs = refs[:count], refs[count:]
    pres, refs = refs[: len(slots)], refs[len(slots) :]
    weight, (out, tokens, stage, sems) = refs[0], refs[-4:]
    if s < 3:
        for piece, row in zip(pieces, rows_of_step(s, place[1])):
            row = pl.multiple_of(row - slots[0] * CHIP, TOK)
            tokens[pl.ds(row, TOK), :] = piece[...]
        grad = dot(tokens[...], weight[...], 1, 1)
    else:
        grad = jnp.concatenate([dot(here[...], weight[...], 1, 1) for here in pieces], axis=0)
    copies = []
    for k, slot in enumerate(slots):
        finish_pre(grad[k * CHIP : (k + 1) * CHIP], pres[k], stage.at[k])
        row = pl.multiple_of(chip_of(slot, place[0]) * CHIP, CHIP)
        copies.append(
            pltpu.make_async_copy(stage.at[k], out.at[:, pl.ds(row, CHIP), :], sems.at[k])
        )
        copies[-1].start()
    for copy in copies:
        copy.wait()


def pre_call(s, place, pieces, pre, weight, so_far=None):
    slots = slots_of_step(s)
    chip = lambda slot: pl.BlockSpec((2, CHIP, UNITS), lambda i, p: (0, chip_of(slot, p[0]), 0))
    any_space = pl.BlockSpec(memory_space=pl.ANY)
    specs = [WHOLE] * len(pieces) + [chip(k) for k in slots] + [WHOLE]
    args = [place, *map(held, pieces), *([pre] * len(slots)), held(weight)]
    aliases = {}
    if so_far is not None:
        aliases = {len(args): 0}
        specs.append(any_space)
        args.append(so_far)
    rows = CHIP * len(slots)
    return pl.pallas_call(
        functools.partial(pre_kernel, s),
        grid_spec=pltpu.PrefetchScalarGridSpec(
            num_scalar_prefetch=1,
            grid=(1,),
            in_specs=specs,
            out_specs=any_space,
            scratch_shapes=[
                pltpu.VMEM((rows, D), BF),
                pltpu.VMEM((len(slots), 2, CHIP, UNITS), BF),
                pltpu.SemaphoreType.DMA((len(slots),)),
            ],
        ),
        out_shape=jax.ShapeDtypeStruct((2, ROWS, UNITS), BF),
        input_output_aliases=aliases,
        compiler_params=params(14),
        cost_estimate=SHORT,
        name="grad_pre",
    )(*args)


def on_device(grad_out, pre_act, down_weight, error, q_start):
    index = lax.axis_index("tensor").astype(jnp.int32)
    place = jnp.stack([index >> 1, index & 1])
    hidden_t = hidden_call(place, pre_act)
    q3 = jnp.concatenate(split_exactly(q_start, 3), axis=0)

    def pre_of(step, pieces, so_far=None):
        return pre_call(step, place, pieces, pre_act, down_weight, so_far)

    a0, b0 = grad_out, other_core(grad_out)
    a1, b1 = along_z(a0), along_z(after(b0, hidden_t))
    grad_pre = pre_of(0, [a0, b0])
    a2 = along_z(after(a1, grad_pre))
    b2 = along_z(after(b1, a1))
    xa1, xb1 = other_core(after(a1, b1)), other_core(after(b1, a1))
    a3 = along_z(after(a2, b1))
    xb1 = after(xb1, a2)
    grad_pre = pre_of(1, [a1, b1, xa1, xb1], grad_pre)
    b3 = along_z(after(b2, a2, grad_pre))
    xa2, xb2 = other_core(after(a2, b2, grad_pre)), other_core(after(b2, a2, grad_pre))
    a4 = along_z(after(a3, b2))
    grad_pre = pre_of(2, [a2, b2, xa2, xb2], grad_pre)
    xa2, xb2, _ = lax.optimization_barrier((xa2, xb2, a3))
    early = [a0, b0, a1, b1, xa1, xb1, a2, b2, xa2, xb2]
    merged, left = main_call(place, early, hidden_t, error, q3)
    xa3, xb3 = other_core(after(a3, b3, left)), other_core(after(b3, a3, left))
    xa4 = other_core(after(a4, b3, left))
    left, last_a = left_call(3, place, [a3, b3, xa3, xb3], hidden_t, q3, left)
    left, last_b = left_call(4, place, [a4, xa4], hidden_t, q3, left)

    lefts = sum_over_ring(left, 0)
    left = sum_of_four(lefts[0], lefts[1], lefts[2], after(lefts[3], grad_pre))
    grad_pre = pre_of(3, [after(last_a, left), last_b], grad_pre)
    lefts = sum_over_ring(left, 1)
    lefts[3] = after(lefts[3], grad_pre)
    p_factor, right = right_call(lefts, hidden_t, last_a, last_b, merged)

    parts = lax.all_to_all(right, "dp", 0, 0, tiled=True)
    lower = merge_call(0, after(hidden_t, right), last_a, last_b, merged)
    summed = sum_call(after(parts, lower))
    right = lax.all_to_all(summed, "dp", 0, 0, tiled=True)
    upper = merge_call(1, after(hidden_t, summed), last_a, last_b, merged)
    new_error, q_factor = error_call(p_factor, lower, upper, right)
    return (grad_pre, new_error, p_factor, q_factor)


def solution(mesh):
    placed = (
        P(("dp", "tensor"), None),
        P(None, "dp", "tensor"),
        P("tensor", None),
        P(("dp", "tensor"), None),
        P("tensor", None),
    )
    return jax.shard_map(
        on_device,
        mesh=mesh,
        in_specs=placed,
        out_specs=(
            P(None, "dp", "tensor"),
            P(("dp", "tensor"), None),
            P(None, "tensor"),
            P("tensor", None),
        ),
        check_vma=False,
    )
```

```python
import functools

import jax
import jax.numpy as jnp
from jax import lax
from jax.experimental import pallas as pl
from jax.experimental.pallas import tpu as pltpu
from jax.sharding import PartitionSpec as P

BF = jnp.bfloat16
F32 = jnp.float32
HI = lax.Precision.HIGHEST
DP = 16
NZ = 8
TOK = 64
CHIP = 2 * TOK
D = 3584
UNITS = 512
ROWS = 1024
EARLY = 5 * CHIP
RANK = 32
BLK = 512
NBLK = D // BLK
MIB = 1024 * 1024


def gelu_pair(value):
    coeff = 0.7978845608028654
    tanh_val = jnp.tanh(coeff * (value + 0.044715 * value * value * value))
    gelu_value = 0.5 * value * (1.0 + tanh_val)
    gelu_slope = 0.5 * (1.0 + tanh_val) + 0.5 * value * (1.0 - tanh_val * tanh_val) * coeff * (
        1.0 + 3.0 * 0.044715 * value * value
    )
    return (gelu_value, gelu_slope)


def split(value, terms):
    parts = []
    for _ in range(terms):
        part = value.astype(BF)
        parts.append(part)
        value = value - part.astype(F32)
    return parts


def split_exactly(value, terms):
    parts = []
    for _ in range(terms):
        part = lax.reduce_precision(value, 8, 7)
        parts.append(part.astype(BF))
        value = value - part
    return parts


def dot(a, b, ca, cb, precision=None):
    return lax.dot_general(
        a, b, (((ca,), (cb,)), ((), ())), preferred_element_type=F32, precision=precision
    )


def fold(stacked, terms):
    total = stacked[0:RANK]
    for k in range(1, terms):
        total = total + stacked[k * RANK : (k + 1) * RANK]
    return total


def chip_of(slot, z):
    return lax.rem(z + jnp.where(slot % 2 == 1, 2 * NZ - (slot + 1) // 2, NZ + slot // 2), NZ)


def rows_of_step(s, core):
    if s == 0:
        return [core * TOK, (1 - core) * TOK]
    if s == 4:
        return [(14 + core) * TOK, (15 - core) * TOK]
    return [
        (4 * s - 2 + 3 * core) * TOK,
        (4 * s - 1 + core) * TOK,
        (4 * s + 1 - 3 * core) * TOK,
        (4 * s - core) * TOK,
    ]


def after(value, *others):
    return lax.optimization_barrier((value,) + others)[0]


def other_core(value):
    return lax.ppermute(value, "tensor", [(i, i ^ 1) for i in range(2 * NZ)])


def along_z(value):
    return lax.ppermute(
        value, "tensor", [(i, (i + 2 - 4 * (i % 2)) % (2 * NZ)) for i in range(2 * NZ)]
    )


def sum_over_ring(value, turn):
    def pairs(k):
        for i in range(DP * 2 * NZ):
            dp, t = divmod(i, 2 * NZ)
            x, y = divmod(dp, 4)
            if (t + turn) % 2 == 0:
                x = (x + k) % 4
            else:
                y = (y + k) % 4
            yield (i, (4 * x + y) * 2 * NZ + t)

    return [value] + [lax.ppermute(value, ("dp", "tensor"), list(pairs(k))) for k in (1, 2, 3)]


def sum_of_four(a, b, c, d):
    return (a + c) + (b + d)


SMEM = pl.BlockSpec(memory_space=pltpu.SMEM)
WHOLE = pl.BlockSpec(memory_space=pltpu.VMEM)


def kept(shape, dtype):
    return pltpu.VMEM(shape, dtype)


def held(value):
    return pltpu.with_memory_space_constraint(value, pltpu.VMEM)


def kept_out(shape, dtype):
    return pltpu.HBM(shape, dtype)


def from_hbm(value):
    return pltpu.with_memory_space_constraint(value, pltpu.HBM)


def params(mib):
    return pltpu.CompilerParams(vmem_limit_bytes=mib * MIB)


def cost(flops, moved):
    return pl.CostEstimate(flops=flops, bytes_accessed=moved, transcendentals=0)


SHORT = cost(10**6, 10**5)


def hidden_kernel(place, pre, hidden_t):
    value, _ = gelu_pair(pre[0].astype(F32))
    hidden = (value * pre[1].astype(F32)).astype(BF).astype(F32)
    hidden_t[...] = jnp.transpose(hidden).astype(BF)


def hidden_call(place, pre):
    return pl.pallas_call(
        hidden_kernel,
        grid_spec=pltpu.PrefetchScalarGridSpec(
            num_scalar_prefetch=1,
            grid=(NZ,),
            in_specs=[pl.BlockSpec((2, CHIP, UNITS), lambda i, p: (0, chip_of(i, p[0]), 0))],
            out_specs=pl.BlockSpec((UNITS, CHIP), lambda i, p: (0, i)),
        ),
        out_shape=kept((UNITS, ROWS), BF),
        compiler_params=params(8),
        cost_estimate=SHORT,
        name="hidden",
    )(place, pre)


def main_kernel(place, *refs):
    pieces = refs[:10]
    hidden_t, error, q3, merged, left, tokens, g_acc, e_acc = refs[10:]
    i = pl.program_id(0)
    rows = [r for s in range(3) for r in rows_of_step(s, place[1])]
    for piece, row in zip(pieces, rows):
        tokens[pl.ds(pl.multiple_of(row, TOK), TOK), :] = piece[...]

    @pl.when(i == 0)
    def _():
        g_acc[...] = jnp.zeros_like(g_acc)
        e_acc[...] = jnp.zeros_like(e_acc)

    block = tokens[...]
    err = error[...]
    merged[...] = (dot(hidden_t[:, :EARLY], block, 1, 0) + err.astype(F32)).astype(BF)
    q = q3[...]
    g_acc[...] += dot(q, block, 1, 1)
    e_acc[...] += dot(q, err, 1, 1)

    @pl.when(i == NBLK - 1)
    def _():
        g = jnp.concatenate(split(fold(g_acc[...], 3), 2), axis=0)
        left[...] = fold(e_acc[...], 3) + fold(dot(g, hidden_t[:, :EARLY], 1, 1), 2)


def main_call(place, pieces, hidden_t, error, q3):
    whole = lambda shape: pl.BlockSpec(shape, lambda i, p: (0, 0))
    cols = lambda rows: pl.BlockSpec((rows, BLK), lambda i, p: (0, i))
    return pl.pallas_call(
        main_kernel,
        grid_spec=pltpu.PrefetchScalarGridSpec(
            num_scalar_prefetch=1,
            grid=(NBLK,),
            in_specs=[cols(TOK)] * 10
            + [whole((UNITS, ROWS)), cols(UNITS), cols(3 * RANK)],
            out_specs=[cols(UNITS), whole((RANK, UNITS))],
            scratch_shapes=[
                pltpu.VMEM((EARLY, BLK), BF),
                pltpu.VMEM((3 * RANK, EARLY), F32),
                pltpu.VMEM((3 * RANK, UNITS), F32),
            ],
        ),
        out_shape=[
            kept((UNITS, D), BF),
            jax.ShapeDtypeStruct((RANK, UNITS), F32),
        ],
        compiler_params=params(14),
        cost_estimate=SHORT,
        name="weight_grad",
    )(place, *map(held, pieces), held(hidden_t), error, q3)


def left_kernel(step, place, *refs):
    pieces = refs[:-5]
    hidden_t, q3, left_in, left, last = refs[-5:]
    base = (5 if step == 3 else 7) * CHIP
    for piece, row in zip(pieces, rows_of_step(step, place[1])):
        last[pl.ds(pl.multiple_of(row - base, TOK), TOK), :] = piece[...]
    g = fold(dot(q3[...], last[...], 1, 1), 3)
    g = jnp.concatenate(split(g, 2), axis=0)
    here = hidden_t[:, base : base + last.shape[0]]
    left[...] = left_in[...] + fold(dot(g, here, 1, 1), 2)


def left_call(step, place, pieces, hidden_t, q3, left_in):
    rows = TOK * len(pieces)
    return pl.pallas_call(
        functools.partial(left_kernel, step),
        in_specs=[SMEM] + [WHOLE] * (len(pieces) + 3),
        out_specs=[WHOLE] * 2,
        out_shape=[
            jax.ShapeDtypeStruct((RANK, UNITS), F32),
            kept((rows, D), BF),
        ],
        compiler_params=params(12),
        cost_estimate=SHORT,
        name="left_of_step",
    )(place, *map(held, pieces), held(hidden_t), held(q3), left_in)


def right_kernel(l0, l1, l2, l3, hidden_t, last_a, last_b, merged, p_out, right):
    left = ((l0[...] + l2[...]) + (l1[...] + l3[...])) * (1.0 / DP)
    rest = dot(left, left, 1, 1, HI)
    rows = lax.broadcasted_iota(jnp.int32, (RANK, RANK), 0)
    inverse = (rows == lax.broadcasted_iota(jnp.int32, (RANK, RANK), 1)).astype(F32)
    for k in range(RANK):
        scale = lax.rsqrt(rest[k : k + 1, k : k + 1])
        column = jnp.where(rows[:, 0:1] > k, rest[:, k : k + 1] * scale, 0.0)
        rest_row = rest[k : k + 1, :] * scale
        inverse_row = inverse[k : k + 1, :] * scale
        rest = rest - column * rest_row
        inverse = jnp.where(rows == k, inverse_row, inverse - column * inverse_row)
    factor = dot(inverse, left, 1, 0, HI)
    p_out[...] = factor
    high, low = split(factor, 2)
    p2 = jnp.concatenate([high, low], axis=0)
    mine = fold(dot(p2, hidden_t[:, EARLY:], 1, 0), 2)
    h2 = jnp.concatenate(split(mine, 2), axis=0)
    for i in range(NBLK):
        c = slice(i * BLK, (i + 1) * BLK)
        total = dot(p2, merged[:, c], 1, 0)
        total += dot(h2[:, : 2 * CHIP], last_a[:, c], 1, 0)
        total += dot(h2[:, 2 * CHIP :], last_b[:, c], 1, 0)
        right[:, :, c] = fold(total, 2).astype(BF).reshape(DP, RANK // DP, BLK)


def right_call(lefts, hidden_t, last_a, last_b, merged):
    return pl.pallas_call(
        right_kernel,
        in_specs=[WHOLE] * 8,
        out_specs=[WHOLE] * 2,
        out_shape=[
            jax.ShapeDtypeStruct((RANK, UNITS), F32),
            jax.ShapeDtypeStruct((DP, RANK // DP, D), BF),
        ],
        compiler_params=params(14),
        cost_estimate=cost(10**8, 8_000_000),
        name="right_factor",
    )(*lefts, held(hidden_t), held(last_a), held(last_b), held(merged))


def sum_kernel(parts, out):
    total = jnp.sum(parts[...].astype(F32), axis=0, keepdims=True)
    out[...] = jnp.broadcast_to(total.astype(BF), out.shape)


def sum_call(parts):
    return pl.pallas_call(
        sum_kernel,
        in_specs=[WHOLE],
        out_specs=WHOLE,
        out_shape=jax.ShapeDtypeStruct(parts.shape, BF),
        compiler_params=params(8),
        cost_estimate=cost(10**6, 500_000),
        name="sum_of_ranks",
    )(parts)


HALF = D // 2
WIDE = HALF // 2


def merge_kernel(hidden_t, last_a, last_b, merged, total):
    part = merged[...].astype(F32)
    part += dot(hidden_t[:, EARLY : EARLY + 2 * CHIP], last_a[...], 1, 0)
    part += dot(hidden_t[:, EARLY + 2 * CHIP :], last_b[...], 1, 0)
    total[...] = part.astype(BF)


def merge_call(half, hidden_t, last_a, last_b, merged):
    place = kept if half else kept_out
    first = half * (HALF // WIDE)
    cols = lambda rows: pl.BlockSpec((rows, WIDE), lambda i: (0, first + i))
    return pl.pallas_call(
        merge_kernel,
        grid=(HALF // WIDE,),
        in_specs=[
            pl.BlockSpec((UNITS, ROWS), lambda i: (0, 0)),
            cols(2 * CHIP),
            cols(CHIP),
            cols(UNITS),
        ],
        out_specs=pl.BlockSpec((UNITS, WIDE), lambda i: (0, i)),
        out_shape=place((UNITS, HALF), BF),
        compiler_params=params(14),
        cost_estimate=cost(3 * CHIP * UNITS * D, 6_000_000),
        name="weight_grad_rest",
    )(*map(from_hbm, (hidden_t, last_a, last_b, merged)))


def error_kernel(factor, lower, upper, summed, out, q, p2_t, low, sem):
    i = pl.program_id(0)
    per = HALF // WIDE
    load = pltpu.make_async_copy(lower, low, sem)

    @pl.when(i == 0)
    def _():
        load.start()
        p2_t[...] = jnp.concatenate(split(jnp.transpose(factor[...]), 2), axis=1)

    mean = summed[...].astype(F32).reshape(RANK, WIDE) * (1.0 / DP)
    q[...] = mean
    rounded = mean.astype(BF)
    rounded = jnp.concatenate([rounded, rounded], axis=0)
    estimate = dot(p2_t[...], rounded, 1, 0)

    @pl.when(i == per)
    def _():
        load.wait()

    for k in range(2 * per):

        @pl.when(i == k)
        def _():
            part = (upper, low)[k // per][:, k % per * WIDE : (k % per + 1) * WIDE]
            out[...] = (part.astype(F32) - estimate).astype(BF)


def error_call(factor, lower, upper, summed):
    per = HALF // WIDE
    turned = lambda i: lax.rem(i + per, 2 * per)
    cols = lambda rows: pl.BlockSpec((rows, WIDE), lambda i: (0, turned(i)))
    return pl.pallas_call(
        error_kernel,
        grid=(D // WIDE,),
        in_specs=[
            pl.BlockSpec((RANK, UNITS), lambda i: (0, 0)),
            pl.BlockSpec(memory_space=pl.ANY),
            WHOLE,
            pl.BlockSpec((DP, RANK // DP, WIDE), lambda i: (0, 0, turned(i))),
        ],
        out_specs=[cols(UNITS), cols(RANK)],
        scratch_shapes=[
            pltpu.VMEM((UNITS, 2 * RANK), BF),
            pltpu.VMEM((UNITS, HALF), BF),
            pltpu.SemaphoreType.DMA,
        ],
        out_shape=[
            jax.ShapeDtypeStruct((UNITS, D), BF),
            jax.ShapeDtypeStruct((RANK, D), F32),
        ],
        compiler_params=params(10),
        cost_estimate=cost(2 * 64 * UNITS * D, 8_000_000),
        name="new_error",
    )(factor, from_hbm(lower), held(upper), summed)


def slots_of_step(s):
    return {0: [0], 3: [5, 6, 7]}.get(s, [2 * s - 1, 2 * s])


def finish_pre(grad, pre, stage):
    value, slope = gelu_pair(pre[0].astype(F32))
    stage[0] = (grad * pre[1].astype(F32) * slope).astype(BF)
    stage[1] = (grad * value).astype(BF)


def pre_kernel(s, place, *refs):
    slots = slots_of_step(s)
    count = 2 if s == 3 else 2 * len(slots)
    pieces, refs = refs[:count], refs[count:]
    pres, refs = refs[: len(slots)], refs[len(slots) :]
    weight, (out, tokens, stage, sems) = refs[0], refs[-4:]
    if s < 3:
        for piece, row in zip(pieces, rows_of_step(s, place[1])):
            row = pl.multiple_of(row - slots[0] * CHIP, TOK)
            tokens[pl.ds(row, TOK), :] = piece[...]
        grad = dot(tokens[...], weight[...], 1, 1)
    else:
        grad = jnp.concatenate([dot(here[...], weight[...], 1, 1) for here in pieces], axis=0)
    copies = []
    for k, slot in enumerate(slots):
        finish_pre(grad[k * CHIP : (k + 1) * CHIP], pres[k], stage.at[k])
        row = pl.multiple_of(chip_of(slot, place[0]) * CHIP, CHIP)
        copies.append(
            pltpu.make_async_copy(stage.at[k], out.at[:, pl.ds(row, CHIP), :], sems.at[k])
        )
        copies[-1].start()
    for copy in copies:
        copy.wait()


def pre_call(s, place, pieces, pre, weight, so_far=None):
    slots = slots_of_step(s)
    chip = lambda slot: pl.BlockSpec((2, CHIP, UNITS), lambda i, p: (0, chip_of(slot, p[0]), 0))
    any_space = pl.BlockSpec(memory_space=pl.ANY)
    specs = [WHOLE] * len(pieces) + [chip(k) for k in slots] + [WHOLE]
    args = [place, *map(held, pieces), *([pre] * len(slots)), held(weight)]
    aliases = {}
    if so_far is not None:
        aliases = {len(args): 0}
        specs.append(any_space)
        args.append(so_far)
    rows = CHIP * len(slots)
    return pl.pallas_call(
        functools.partial(pre_kernel, s),
        grid_spec=pltpu.PrefetchScalarGridSpec(
            num_scalar_prefetch=1,
            grid=(1,),
            in_specs=specs,
            out_specs=any_space,
            scratch_shapes=[
                pltpu.VMEM((rows, D), BF),
                pltpu.VMEM((len(slots), 2, CHIP, UNITS), BF),
                pltpu.SemaphoreType.DMA((len(slots),)),
            ],
        ),
        out_shape=jax.ShapeDtypeStruct((2, ROWS, UNITS), BF),
        input_output_aliases=aliases,
        compiler_params=params(14),
        cost_estimate=SHORT,
        name="grad_pre",
    )(*args)


def on_device(grad_out, pre_act, down_weight, error, q_start):
    index = lax.axis_index("tensor").astype(jnp.int32)
    place = jnp.stack([index >> 1, index & 1])
    hidden_t = hidden_call(place, pre_act)
    q3 = jnp.concatenate(split_exactly(q_start, 3), axis=0)

    def pre_of(step, pieces, so_far=None):
        return pre_call(step, place, pieces, pre_act, down_weight, so_far)

    a0, b0 = grad_out, other_core(grad_out)
    a1, b1 = along_z(a0), along_z(after(b0, hidden_t))
    grad_pre = pre_of(0, [a0, b0])
    a2 = along_z(after(a1, grad_pre))
    b2 = along_z(after(b1, a1))
    xa1, xb1 = other_core(after(a1, b1)), other_core(after(b1, a1))
    a3 = along_z(after(a2, b1))
    xb1 = after(xb1, a2)
    grad_pre = pre_of(1, [a1, b1, xa1, xb1], grad_pre)
    b3 = along_z(after(b2, a2, grad_pre))
    xa2, xb2 = other_core(after(a2, b2, grad_pre)), other_core(after(b2, a2, grad_pre))
    a4 = along_z(after(a3, b2, xa2))
    grad_pre = pre_of(2, [a2, b2, xa2, xb2], grad_pre)
    xa2, xb2, _ = lax.optimization_barrier((xa2, xb2, a3))
    early = [a0, b0, a1, b1, xa1, xb1, a2, b2, xa2, xb2]
    merged, left = main_call(place, early, hidden_t, error, q3)
    xa3, xb3 = other_core(after(a3, b3, left)), other_core(after(b3, a3, left))
    xa4 = other_core(after(a4, b3, left))
    left, last_a = left_call(3, place, [a3, b3, xa3, xb3], hidden_t, q3, left)
    left, last_b = left_call(4, place, [a4, xa4], hidden_t, q3, left)

    lefts = sum_over_ring(left, 0)
    left = sum_of_four(lefts[0], lefts[1], lefts[2], after(lefts[3], grad_pre))
    grad_pre = pre_of(3, [after(last_a, left), last_b], grad_pre)
    lefts = sum_over_ring(left, 1)
    lefts[3] = after(lefts[3], grad_pre)
    p_factor, right = right_call(lefts, hidden_t, last_a, last_b, merged)

    parts = lax.all_to_all(right, "dp", 0, 0, tiled=True)
    lower = merge_call(0, after(hidden_t, right), last_a, last_b, merged)
    summed = sum_call(after(parts, lower))
    right = lax.all_to_all(summed, "dp", 0, 0, tiled=True)
    upper = merge_call(1, after(hidden_t, summed), last_a, last_b, merged)
    new_error, q_factor = error_call(p_factor, lower, upper, right)
    return (grad_pre, new_error, p_factor, q_factor)


def solution(mesh):
    placed = (
        P(("dp", "tensor"), None),
        P(None, "dp", "tensor"),
        P("tensor", None),
        P(("dp", "tensor"), None),
        P("tensor", None),
    )
    return jax.shard_map(
        on_device,
        mesh=mesh,
        in_specs=placed,
        out_specs=(
            P(None, "dp", "tensor"),
            P(("dp", "tensor"), None),
            P(None, "tensor"),
            P("tensor", None),
        ),
        check_vma=False,
    )
```
